512 devices in a mesh: dom: 64 (over y_hi, z, core), blk: 8 (over x, y_lo).
Axes of the slice: x: 4, y: 8 (y_hi: 4, y_lo: 2; y = y_hi * 2 + y_lo), z: 8, core: 2. Of those that a mesh axis runs over, the one named last changes fastest.
Arguments:
- features: bfloat16 [65536, 128], P(('dom', 'blk')), may hold values from -6 to 6
- weight: bfloat16 [128, 256], replicated, may hold values from -0.5 to 0.5
- out_bias: float32 [256], replicated, may hold values from -4 to 4
- degree: int32 [65536], P(('dom', 'blk')), may hold values from 1 to 64
- edge_dst: int32 [512, 8, 384], P('dom', 'blk'), may hold values from 0 to 128, as said below
- edge_src: int32 [512, 8, 384], P('dom', 'blk'), may hold values from 0 to 127
- hub_rows: int32 [64, 8, 64, 64], P('dom', 'blk'), may hold values from 0 to 127
- hub_count: int32 [64, 8, 64], P('dom', 'blk'), may hold values from 1 to 64, as said below
- hub_target: int32 [64, 8, 64, 64], P('dom', 'blk'), may hold values from 0 to 127
- cotangent: bfloat16 [65536, 256], P(('dom', 'blk')), may hold values from -6 to 6
Outputs:
- activated: bfloat16 [65536, 256], P(('dom', 'blk'))
- grad_features: bfloat16 [65536, 128], P(('dom', 'blk'))
- grad_weight: float32 [128, 256], replicated
- grad_bias: float32 [256], replicated
The draws below stay inside these ranges and needn't reach their ends.
Inputs may be any that keep to these rules, and one draw needn't show every extreme that they name: `edge_dst`: each list ends in 1 to 192 padding entries equal to 128; all other entries are below 128. `hub_count`: for every source partition and member, some destination partition receives all 64 slots.
All inputs are finite; a program needn't handle non-finite values.
Results may differ from the reference program's by a relative error of at most 0.0085.
Values may be sent and summed in bfloat16 or wider, within the bound.
A program may use at most 64 MiB of HBM per device.

```python
import jax
import jax.numpy as jnp
from jax import lax

F_IN = 128
H = 256
TILE = 128
ROWS_DEV = 128
EB = 384
HUB = 64
SRC_BLOCKS = 1
DST_BLOCKS = 8
ROWS_GRP = 1024
NODES = 65536
N_DOM = 64
N_BLK = 8


def draw_edge_dst(key, part):
    key = jax.random.fold_in(key, 11)
    key_vals, key_pad = jax.random.split(key)
    shape = (N_DOM * DST_BLOCKS, N_BLK * SRC_BLOCKS, EB)
    values = jax.random.randint(key_vals, shape, 0, TILE, dtype=jnp.int32)
    padding = jax.random.randint(key_pad, (shape[0], shape[1], 1), 1, EB // 2 + 1, dtype=jnp.int32)
    slot_ids = jnp.arange(EB, dtype=jnp.int32)[None, None, :]
    return jnp.where(slot_ids >= EB - padding, TILE, values).astype(jnp.int32)


def draw_hub_count(key, part):
    key = jax.random.fold_in(key, 23)
    key_counts, key_full = jax.random.split(key)
    shape = (N_DOM, N_BLK, N_DOM)
    counts = jax.random.randint(key_counts, shape, 1, HUB + 1, dtype=jnp.int32)
    full_dest = jax.random.randint(key_full, (N_DOM, N_BLK, 1), 0, N_DOM, dtype=jnp.int32)
    dest_ids = jnp.arange(N_DOM, dtype=jnp.int32)[None, None, :]
    return jnp.where(dest_ids == full_dest, HUB, counts).astype(jnp.int32)


def set_ends(array, key, low, high):
    extent = array.shape
    place = [jax.random.randint(jax.random.fold_in(key, axis), (), 0, extent[axis]) for axis in range(len(extent))]
    array = array.at[tuple(place)].set(low)
    longest = extent.index(max(extent))
    place[longest] = (place[longest] + 1) % extent[longest]
    return array.at[tuple(place)].set(high)


def level_of(own_key, extent, cuts, least, high):
    gain = 1.0
    for position, blocks in cuts:
        heights = jax.random.uniform(jax.random.fold_in(jax.random.fold_in(own_key, 6), position), (blocks,), jnp.float32, least / len(cuts), high / len(cuts))
        gain = gain * jnp.repeat(jnp.exp(heights), extent[position] // blocks).reshape((-1,) + (1,) * (len(extent) - 1 - position))
    return gain


def noise(own_key, extent, spread, reach, shards=(), held_as=jnp.bfloat16):
    entries = jax.random.normal(own_key, extent, jnp.float32) * spread
    if len(shards) > 0:
        entries = level_of(own_key, extent, shards, -0.22, 0.18) * entries
    return jnp.clip(entries, min=-reach, max=reach).astype(held_as)


def setup_inputs(seed: int = 0) -> dict:
    seeds = jax.random.split(jax.random.key(seed), 11)
    features = noise(seeds[0], (NODES, F_IN), 1.0, 6.0, ((0, 512),))
    weight = noise(seeds[1], (F_IN, H), F_IN ** -0.5, 0.5)
    out_bias = noise(seeds[2], (H,), 1.0, 4.0, (), jnp.float32)
    degree = set_ends(jax.random.randint(seeds[3], (NODES,), 1, 65), jax.random.fold_in(seeds[3], 1), 1, 64).astype(jnp.int32)
    edge_dst = draw_edge_dst(jax.random.fold_in(seeds[10], 71), 0)
    edge_src = set_ends(jax.random.randint(seeds[5], (N_DOM * DST_BLOCKS, N_BLK * SRC_BLOCKS, EB), 0, TILE), jax.random.fold_in(seeds[5], 1), 0, TILE - 1).astype(jnp.int32)
    hub_rows = set_ends(jax.random.randint(seeds[6], (N_DOM, N_BLK, N_DOM, HUB), 0, ROWS_DEV), jax.random.fold_in(seeds[6], 1), 0, ROWS_DEV - 1).astype(jnp.int32)
    hub_count = draw_hub_count(jax.random.fold_in(seeds[10], 71), 0)
    hub_target = set_ends(jax.random.randint(seeds[8], (N_DOM, N_BLK, N_DOM, HUB), 0, ROWS_DEV), jax.random.fold_in(seeds[8], 1), 0, ROWS_DEV - 1).astype(jnp.int32)
    cotangent = noise(seeds[9], (NODES, H), 1.0, 6.0, ((0, 512),))
    return dict(features=features, weight=weight, out_bias=out_bias, degree=degree, edge_dst=edge_dst, edge_src=edge_src, hub_rows=hub_rows, hub_count=hub_count, hub_target=hub_target, cotangent=cotangent)


def group_counts(dst_lists, src_lists):
    blocks = dst_lists.shape[0]
    block_row = jnp.arange(blocks, dtype=jnp.int32)[:, None, None]
    block_col = jnp.arange(blocks, dtype=jnp.int32)[None, :, None]
    row_index = jnp.where(dst_lists < TILE, block_row * TILE + dst_lists, blocks * TILE).astype(jnp.int32)
    col_index = jnp.broadcast_to(block_col * TILE + src_lists, row_index.shape).astype(jnp.int32)
    empty = jnp.zeros((blocks * TILE, blocks * TILE), jnp.float32)
    return empty.at[row_index, col_index].add(1.0, mode='drop')

def group_product(dst_groups, src_groups, values, transposed):

    def one_group(items):
        dst_one, src_one, val_one = items
        counts = group_counts(dst_one, src_one)
        if transposed:
            counts = counts.T
        return jnp.dot(counts.astype(jnp.bfloat16), val_one, preferred_element_type=jnp.float32)
    return lax.map(one_group, (dst_groups, src_groups, values))

def member_sum(member_values, member_rows):
    return jax.ops.segment_sum(member_values.reshape(-1, member_values.shape[-1]), member_rows.reshape(-1), num_segments=ROWS_DEV)

def hub_forward(projected, hub_rows, hub_count, hub_target):
    source_view = projected.reshape(N_DOM, N_BLK, ROWS_DEV, H)
    slot_ids = jnp.arange(HUB, dtype=jnp.int32)

    def receive(partition):
        picked_rows = hub_rows[:, :, partition, :]
        values = jnp.take_along_axis(source_view, picked_rows[..., None], axis=2).astype(jnp.float32)
        live_slots = slot_ids[None, None, :] < hub_count[:, :, partition][..., None]
        values = jnp.where(live_slots[..., None], values, jnp.float32(0.0))
        values = jnp.transpose(values, (1, 0, 2, 3))
        return jax.vmap(member_sum)(values, hub_target[partition])
    received = lax.map(receive, jnp.arange(N_DOM, dtype=jnp.int32))
    return received.reshape(NODES, H)

def hub_backward(back_scaled, weight, hub_rows, hub_count, hub_target):
    reader_view = back_scaled.reshape(N_DOM, N_BLK, ROWS_DEV, H)
    slot_ids = jnp.arange(HUB, dtype=jnp.int32)
    weight_wide = weight.astype(jnp.float32)

    def send_back(partition):
        picked_rows = hub_target[:, :, partition, :]
        picked = jnp.take_along_axis(reader_view, picked_rows[..., None], axis=2)
        slot_grad = jnp.einsum('abkh,fh->abkf', picked.astype(jnp.float32), weight_wide).astype(jnp.bfloat16)
        slot_grad = lax.optimization_barrier(slot_grad).astype(jnp.float32)
        values = jnp.transpose(picked.astype(jnp.float32), (1, 0, 2, 3))
        slot_grad = jnp.transpose(slot_grad, (1, 0, 2, 3))
        live_slots = slot_ids[None, None, :] < hub_count[partition][..., None]
        values = jnp.where(live_slots[..., None], values, jnp.float32(0.0))
        slot_grad = jnp.where(live_slots[..., None], slot_grad, jnp.float32(0.0))
        return (jax.vmap(member_sum)(values, hub_rows[partition]), jax.vmap(member_sum)(slot_grad, hub_rows[partition]))
    returned, input_back = lax.map(send_back, jnp.arange(N_DOM, dtype=jnp.int32))
    return (returned.reshape(NODES, H), input_back.reshape(NODES, F_IN))

def reference(features, weight, out_bias, degree, edge_dst, edge_src, hub_rows, hub_count, hub_target, cotangent):
    row_scale = lax.rsqrt(degree.astype(jnp.float32))[:, None]
    projected = (row_scale * jnp.dot(features, weight, preferred_element_type=jnp.float32)).astype(jnp.bfloat16)
    dst_groups = edge_dst.reshape(N_DOM, DST_BLOCKS, DST_BLOCKS, EB)
    src_groups = edge_src.reshape(N_DOM, DST_BLOCKS, DST_BLOCKS, EB)
    local_sum = group_product(dst_groups, src_groups, projected.reshape(N_DOM, ROWS_GRP, H), False).reshape(NODES, H)
    hub_sum = hub_forward(projected, hub_rows, hub_count, hub_target)
    pre_act = row_scale * (local_sum + hub_sum) + out_bias[None, :]
    activated = jax.nn.silu(pre_act).astype(jnp.bfloat16)
    sigmoid_val = jax.nn.sigmoid(pre_act)
    grad_pre = cotangent.astype(jnp.float32) * sigmoid_val * (1.0 + pre_act * (1.0 - sigmoid_val))
    grad_bias = lax.optimization_barrier(jnp.sum(grad_pre, axis=0))
    back_scaled = (row_scale * grad_pre).astype(jnp.bfloat16)
    back_local = group_product(dst_groups, src_groups, back_scaled.reshape(N_DOM, ROWS_GRP, H), True).reshape(NODES, H)
    back_hub, hub_input_back = hub_backward(back_scaled, weight, hub_rows, hub_count, hub_target)
    grad_local = (row_scale * back_local).astype(jnp.bfloat16)
    grad_features = (jnp.dot(grad_local, weight.T, preferred_element_type=jnp.float32) + row_scale * hub_input_back).astype(jnp.bfloat16)
    grad_weight = jnp.dot(features.T, grad_local, preferred_element_type=jnp.float32)
    grad_weight = grad_weight + jnp.dot(features.T.astype(jnp.float32), row_scale * back_hub, precision=lax.Precision.HIGHEST)
    return (activated, grad_features, grad_weight, grad_bias)
```

```python
import functools

import jax
import jax.numpy as jnp
from jax import lax
from jax.experimental import pallas as pl
from jax.experimental.pallas import tpu as pltpu
from jax.sharding import PartitionSpec as P

F32 = jnp.float32
BF16 = jnp.bfloat16
NT = (((1,), (1,)), ((), ()))
YH, ZN, CN, NB = 4, 8, 2, 8
ROWS, FIN, HID, HUB, EB = 128, 128, 256, 64, 384


def iota(shape, dim):
    return lax.broadcasted_iota(jnp.int32, shape, dim)


def mod(value, size):
    return lax.rem(value + size, size)


def column(row):
    n = row.shape[1]
    wide = jnp.broadcast_to(row.astype(F32), (n, n))
    return jnp.sum(jnp.where(iota((n, n), 0) == iota((n, n), 1), wide, 0.0), axis=1, keepdims=True)


def hot(row, size):
    return (iota((size, row.shape[1]), 0) == row).astype(F32).astype(BF16)


def kernel(
    feat_ref, weight_ref, bias_ref, degree_ref, dst_ref, src_ref, rows_ref, count_ref, target_ref, cot_ref,
    act_ref, gfeat_ref, gw_ref, gb_ref,
    xall, gall, acc, counts, counts_t, psend, precv, gblk, sendtab, loctab, mid, tab,
    w1s, w1r, w2s, w2r, w3r,
    xs_send, xs_recv, gs_send, gs_recv, p_send, p_recv, q_send, q_recv,
    i1_send, i1_recv, i2_send, i2_recv, w1_send, w1_recv, w2_send, w2_recv, w3_send, w3_recv,
):
    dom = lax.axis_index("dom")
    blk = lax.axis_index("blk")
    c = lax.rem(dom, CN)
    z = lax.rem(lax.div(dom, CN), ZN)
    y = lax.div(dom, CN * ZN)

    def at(yy, zz, cc):
        return (yy * ZN + zz) * CN + cc

    def remote(src, dst, send, recv, to_dom, to_blk):
        return pltpu.make_async_remote_copy(
            src_ref=src, dst_ref=dst, send_sem=send, recv_sem=recv,
            device_id=(to_dom, to_blk), device_id_type=pl.DeviceIdType.MESH,
        )

    barrier = pltpu.get_barrier_semaphore()

    def greet(to_dom, to_blk):
        pl.semaphore_signal(barrier, inc=1, device_id=(to_dom, to_blk), device_id_type=pl.DeviceIdType.MESH)

    def greet_a(i, carry):
        a = mod(blk * CN + c + i, NB * CN)
        greet(at(y, z, lax.rem(a, CN)), lax.div(a, CN))
        return carry

    def greet_b(i, carry):
        b = mod(y * ZN + z + i, YH * ZN)
        greet(b * CN + c, blk)
        return carry

    lax.fori_loop(1, NB * CN, greet_a, 0)
    lax.fori_loop(1, YH * ZN, greet_b, 0)
    for i in range(1, YH):
        greet(at(mod(y + i, YH), z, 1 - c), blk)

    scale = lax.rsqrt(column(degree_ref[...]))
    xs = (scale * feat_ref[...].astype(F32)).astype(BF16)
    xall[dom] = xs

    live = iota((HUB, HUB), 1).astype(F32) < column(count_ref[0])
    rows = jnp.where(live, rows_ref[0, 0], ROWS)
    target = target_ref[0, 0]
    mid_tab = jnp.concatenate([rows, target], axis=1)
    loctab[...] = jnp.concatenate([target, rows], axis=1)
    for e in range(YH * ZN * CN):
        sendtab[e // 16, (e // 2) % 8, e % 2] = mid_tab[e : e + 1, :]

    pl.semaphore_wait(barrier, (NB * CN - 1) + (YH * ZN - 1) + (YH - 1))

    def block_copy(buf, send, recv, e, k, to_dom):
        return remote(buf.at[e], buf.at[e], send.at[k], recv.at[e], to_dom, blk)

    def own_sends(buf, send, recv):
        return [
            block_copy(buf, send, recv, dom, 0, at(y, mod(z + 1, ZN), c)),
            block_copy(buf, send, recv, dom, 1, at(y, mod(z - 1, ZN), c)),
            block_copy(buf, send, recv, dom, 2, at(mod(y + 1, YH), z, c)),
            block_copy(buf, send, recv, dom, 3, at(mod(y - 1, YH), z, c)),
            block_copy(buf, send, recv, dom, 4, at(mod(y + 2, YH), z, c)),
            block_copy(buf, send, recv, dom, 5, at(y, z, 1 - c)),
        ]

    def y_block(t):
        return jnp.where(t == 0, 3, t)

    def dy_of(k):
        return jnp.where(k == 0, 0, y_block(k - 1))

    def far_sign(k):
        return jnp.where(k < 2, 1, -1)

    def gather_loop(buf, send, recv, extra, forward):
        def contribution(m):
            pieces = []
            for cc in range(CN):
                e = m * CN + cc
                lanes = iota((1, 2 * HUB), 1)
                mine = jnp.where((lanes < HUB) == forward, loctab[pl.ds(e, 1), :], -1)
                theirs = tab[lax.div(m, ZN), lax.rem(m, ZN), cc]
                pieces.append(
                    lax.dot_general(hot(mine, ROWS), hot(theirs, ROWS), NT, preferred_element_type=F32).astype(BF16)
                )
            joint = jnp.concatenate(pieces, axis=1)
            return jnp.dot(joint, buf[pl.ds(m * CN, CN)].reshape(CN * ROWS, FIN), preferred_element_type=F32)

        def wait_block(e):
            block_copy(buf, send, recv, e, 0, dom).wait_recv()

        def step(t, carry):
            k = lax.rem(t, 4)
            s = lax.div(t, 4) + 1

            @pl.when(t < 3)
            def _():
                e = at(mod(y + y_block(t), YH), z, c)
                wait_block(e)
                block_copy(buf, send, recv, e, 6 + 3 * t, at(y, mod(z + 1, ZN), c)).start()
                block_copy(buf, send, recv, e, 7 + 3 * t, at(y, mod(z - 1, ZN), c)).start()
                block_copy(buf, send, recv, e, 8 + 3 * t, at(y, z, 1 - c)).start()

            @pl.when(t < 16)
            def _():
                for slot, sign in ((0, 1), (1, -1)):
                    far = far_sign(k) == sign

                    @pl.when((s < 4) | far)
                    def _():
                        e = at(mod(y + dy_of(k), YH), mod(z - sign * s, ZN), c)
                        wait_block(e)

                        @pl.when((s < 3) | ((s == 3) & far))
                        def _():
                            block_copy(buf, send, recv, e, 15 + 4 * t + slot, at(y, mod(z + sign, ZN), c)).start()

                        block_copy(buf, send, recv, e, 17 + 4 * t + slot, at(y, z, 1 - c)).start()

            extra(t)

            @pl.when(t < 4)
            def _():
                m = mod(y + dy_of(t), YH) * ZN + z
                wait_block(m * CN + 1 - c)
                acc[...] += contribution(m)

            prev = t - 1
            pk = lax.rem(prev + 4, 4)
            ps = lax.div(prev, 4) + 1
            row = mod(y + dy_of(pk), YH) * ZN

            @pl.when((t >= 1) & (t <= 12))
            def _():
                up = row + mod(z - ps, ZN)
                down = row + mod(z + ps, ZN)
                wait_block(up * CN + 1 - c)
                wait_block(down * CN + 1 - c)
                acc[...] += contribution(up) + contribution(down)

            @pl.when(t > 12)
            def _():
                m = row + mod(z + 4, ZN)
                wait_block(m * CN + 1 - c)
                acc[...] += contribution(m)

            return carry

        lax.fori_loop(0, 17, step, 0)

    def gather_finish(buf, send, recv):
        for k in range(6):
            block_copy(buf, send, recv, dom, k, dom).wait_send()

        def drain_y(t, carry):
            for i in range(3):
                block_copy(buf, send, recv, dom, 6 + 3 * t + i, dom).wait_send()
            return carry

        def drain(t, carry):
            k = lax.rem(t, 4)
            s = lax.div(t, 4) + 1
            for slot, sign in ((0, 1), (1, -1)):
                far = far_sign(k) == sign

                @pl.when((s < 3) | ((s == 3) & far))
                def _():
                    block_copy(buf, send, recv, dom, 15 + 4 * t + slot, dom).wait_send()

                @pl.when((s < 4) | far)
                def _():
                    block_copy(buf, send, recv, dom, 17 + 4 * t + slot, dom).wait_send()

            return carry

        lax.fori_loop(0, 3, drain_y, 0)
        lax.fori_loop(0, 16, drain, 0)

    for copy in own_sends(xall, xs_send, xs_recv):
        copy.start()

    def table_z(i):
        zz = mod(z + i, ZN)
        return remote(sendtab.at[:, zz], mid.at[:, :, z], i1_send.at[i], i1_recv.at[z], at(y, zz, c), blk)

    def table_z_in(i):
        zz = mod(z + i, ZN)
        return remote(sendtab.at[:, zz], mid.at[:, :, zz], i1_send.at[i], i1_recv.at[zz], at(y, zz, c), blk)

    def table_yc(i):
        other = mod(y * CN + c + i, YH * CN)
        yy, cc = lax.div(other, CN), lax.rem(other, CN)
        return remote(
            mid.at[yy, cc], tab.at[y, :, c], i2_send.at[i], i2_recv.at[y * CN + c], at(yy, z, cc), blk
        )

    def table_yc_in(i):
        other = mod(y * CN + c + i, YH * CN)
        yy, cc = lax.div(other, CN), lax.rem(other, CN)
        return remote(mid.at[yy, cc], tab.at[yy, :, cc], i2_send.at[i], i2_recv.at[other], at(yy, z, cc), blk)

    for i in range(1, ZN):
        table_z(i).start()
    for yy in range(YH):
        for cc in range(CN):
            mid[yy, cc, z] = sendtab[yy, z, cc]
    for i in range(1, ZN):
        table_z_in(i).wait_recv()
    for i in range(1, YH * CN):
        table_yc(i).start()
    for zz in range(ZN):
        tab[y, zz, c] = mid[y, c, zz]

    acc[...] = jnp.zeros_like(acc)

    def part_copy(a, to_blk, came):
        return remote(psend.at[a], precv.at[came], p_send.at[a], p_recv.at[came], dom, to_blk)

    def forward_extra(t):
        @pl.when(t < NB)
        def _():
            a = mod(blk + 1 + t, NB)
            dst_hot = hot(dst_ref[a], ROWS)
            src_hot = hot(src_ref[a], ROWS)
            count = lax.dot_general(dst_hot, src_hot, NT, preferred_element_type=F32).astype(BF16)
            count_t = lax.dot_general(src_hot, dst_hot, NT, preferred_element_type=F32).astype(BF16)
            counts_t[a] = count_t
            part = jnp.dot(count, xall[dom], preferred_element_type=F32)

            @pl.when(a != blk)
            def _():
                psend[a] = part.astype(BF16)
                part_copy(a, a, blk).start()

            @pl.when(a == blk)
            def _():
                counts[...] = part

        @pl.when(t == 0)
        def _():
            for i in range(1, YH * CN):
                table_yc_in(i).wait_recv()

    gather_loop(xall, xs_send, xs_recv, forward_extra, True)

    total = acc[...] + counts[...]
    for i in range(1, NB):
        other = mod(blk + i, NB)
        part_copy(other, other, other).wait_recv()
        total = total + precv[other].astype(F32)

    weight = weight_ref[...]
    pre = scale * jnp.dot(total.astype(BF16), weight, preferred_element_type=F32) + bias_ref[...]
    sig = jax.nn.sigmoid(pre)
    act_ref[...] = (pre * sig).astype(BF16)
    grad_pre = cot_ref[...].astype(F32) * sig * (1.0 + pre * (1.0 - sig))
    back = (scale * grad_pre).astype(BF16)
    grad = lax.dot_general(back, weight, NT, preferred_element_type=F32).astype(BF16)
    gall[dom] = grad
    for copy in own_sends(gall, gs_send, gs_recv):
        copy.start()

    gblk[blk] = grad

    def member_copy(i, came):
        other = mod(blk + i, NB)
        return remote(gall.at[dom], gblk.at[came], q_send.at[i], q_recv.at[came], dom, other)

    for i in range(1, NB):
        member_copy(i, blk).start()

    bias_term = jnp.sum(grad_pre, axis=0, keepdims=True)
    gw = jnp.dot(total.T.astype(BF16), back, preferred_element_type=F32)
    me_a = blk * CN + c
    me_b = y * ZN + z
    for a in range(NB * CN):
        w1s[a, 0:8, :] = gw[8 * a : 8 * a + 8, 0:128]
        w1s[a, 8:16, :] = gw[8 * a : 8 * a + 8, 128:256]
        w1s[a, 16:17, :] = bias_term[:, 0:128]
        w1s[a, 17:18, :] = bias_term[:, 128:256]
    w1r[me_a] = w1s[me_a]

    def w1_copy(i, incoming):
        a = mod(me_a + i, NB * CN)
        came = a if incoming else me_a
        return remote(
            w1s.at[a], w1r.at[came], w1_send.at[i], w1_recv.at[came], at(y, z, lax.rem(a, CN)), lax.div(a, CN)
        )

    def w2_copy(i, incoming):
        b = mod(me_b + i, YH * ZN)
        came = b if incoming else me_b
        return remote(w2s, w2r.at[came], w2_send.at[i], w2_recv.at[came], b * CN + c, blk)

    def w3_copy(i, incoming):
        a = mod(me_a + i, NB * CN)
        came = a if incoming else me_a
        return remote(
            w3r.at[came], w3r.at[came], w3_send.at[i], w3_recv.at[came], at(y, z, lax.rem(a, CN)), lax.div(a, CN)
        )

    def each(count, body):
        def run(i, carry):
            body(i)
            return carry

        lax.fori_loop(1, count, run, 0)

    each(NB * CN, lambda i: w1_copy(i, False).start())

    acc[...] = jnp.zeros_like(acc)

    def backward_extra(t):
        @pl.when(t == 3)
        def _():
            each(NB * CN, lambda i: w1_copy(i, True).wait_recv())
            w2s[...] = jnp.sum(w1r[...], axis=0)
            w2r[me_b] = w2s[...]
            each(YH * ZN, lambda i: w2_copy(i, False).start())

        @pl.when(t == 9)
        def _():
            each(YH * ZN, lambda i: w2_copy(i, True).wait_recv())
            w3r[me_a] = jnp.sum(w2r[...], axis=0)
            each(NB * CN, lambda i: w3_copy(i, False).start())

    gather_loop(gall, gs_send, gs_recv, backward_extra, False)

    total_back = acc[...]
    for i in range(1, NB):
        member_copy(i, mod(blk + i, NB)).wait_recv()
    for a in range(NB):
        total_back = total_back + jnp.dot(counts_t[a], gblk[a], preferred_element_type=F32)
    gfeat_ref[...] = (scale * total_back).astype(BF16)

    each(NB * CN, lambda i: w3_copy(i, True).wait_recv())
    for a in range(NB * CN):
        gw_ref[8 * a : 8 * a + 8, 0:128] = w3r[a, 0:8, :]
        gw_ref[8 * a : 8 * a + 8, 128:256] = w3r[a, 8:16, :]
    gb_ref[...] = w3r[me_a, 16:18, :]

    gather_finish(xall, xs_send, xs_recv)
    gather_finish(gall, gs_send, gs_recv)
    for i in range(1, ZN):
        table_z(i).wait_send()
    for i in range(1, YH * CN):
        table_yc(i).wait_send()
    for i in range(1, NB):
        other = mod(blk + i, NB)
        part_copy(other, other, blk).wait_send()
        member_copy(i, blk).wait_send()
    each(NB * CN, lambda i: w1_copy(i, False).wait_send())
    each(YH * ZN, lambda i: w2_copy(i, False).wait_send())
    each(NB * CN, lambda i: w3_copy(i, False).wait_send())


def per_device(features, weight, out_bias, degree, edge_dst, edge_src, hub_rows, hub_count, hub_target, cotangent):
    nd = YH * ZN * CN
    vmem = pl.BlockSpec(memory_space=pltpu.VMEM)
    dma = pltpu.SemaphoreType.DMA
    act, gfeat, gw, gb = pl.pallas_call(
        kernel,
        out_shape=(
            jax.ShapeDtypeStruct((ROWS, HID), BF16),
            jax.ShapeDtypeStruct((ROWS, FIN), BF16),
            jax.ShapeDtypeStruct((FIN, HID), F32),
            jax.ShapeDtypeStruct((2, 128), F32),
        ),
        in_specs=[vmem] * 10,
        out_specs=(vmem,) * 4,
        scratch_shapes=[
            pltpu.VMEM((nd, ROWS, FIN), BF16),
            pltpu.VMEM((nd, ROWS, FIN), BF16),
            pltpu.VMEM((ROWS, FIN), F32),
            pltpu.VMEM((ROWS, FIN), F32),
            pltpu.VMEM((NB, ROWS, ROWS), BF16),
            pltpu.VMEM((NB, ROWS, FIN), BF16),
            pltpu.VMEM((NB, ROWS, FIN), BF16),
            pltpu.VMEM((NB, ROWS, FIN), BF16),
            pltpu.VMEM((YH, ZN, CN, 1, 2 * HUB), jnp.int32),
            pltpu.VMEM((nd, 2 * HUB), jnp.int32),
            pltpu.VMEM((YH, CN, ZN, 1, 2 * HUB), jnp.int32),
            pltpu.VMEM((YH, ZN, CN, 1, 2 * HUB), jnp.int32),
            pltpu.VMEM((NB * CN, 18, 128), F32),
            pltpu.VMEM((NB * CN, 18, 128), F32),
            pltpu.VMEM((18, 128), F32),
            pltpu.VMEM((YH * ZN, 18, 128), F32),
            pltpu.VMEM((NB * CN, 18, 128), F32),
            dma((80,)), dma((nd,)), dma((80,)), dma((nd,)),
            dma((NB,)), dma((NB,)), dma((NB,)), dma((NB,)),
            dma((ZN,)), dma((ZN,)), dma((YH * CN,)), dma((YH * CN,)),
            dma((NB * CN,)), dma((NB * CN,)), dma((YH * ZN,)), dma((YH * ZN,)), dma((NB * CN,)), dma((NB * CN,)),
        ],
        compiler_params=pltpu.CompilerParams(
            collective_id=0, has_side_effects=True, vmem_limit_bytes=24 * 1024 * 1024
        ),
    )(
        features, weight, out_bias.reshape(1, HID), degree.reshape(1, ROWS), edge_dst, edge_src,
        hub_rows, hub_count, hub_target, cotangent,
    )
    return act, gfeat, gw, gb.reshape(HID)


def solution(mesh):
    return jax.shard_map(
        per_device,
        mesh=mesh,
        in_specs=(
            P(("dom", "blk"), None),
            P(),
            P(),
            P(("dom", "blk")),
            P("dom", "blk", None),
            P("dom", "blk", None),
            P("dom", "blk", None, None),
            P("dom", "blk", None),
            P("dom", "blk", None, None),
            P(("dom", "blk"), None),
        ),
        out_specs=(P(("dom", "blk"), None), P(("dom", "blk"), None), P(), P()),
        check_vma=False,
    )
```

```python
import functools

import jax
import jax.numpy as jnp
from jax import lax
from jax.experimental import pallas as pl
from jax.experimental.pallas import tpu as pltpu
from jax.sharding import PartitionSpec as P

F32 = jnp.float32
BF16 = jnp.bfloat16
NT = (((1,), (1,)), ((), ()))
YH, ZN, CN, NB = 4, 8, 2, 8
ROWS, FIN, HID, HUB, EB = 128, 128, 256, 64, 384


def iota(shape, dim):
    return lax.broadcasted_iota(jnp.int32, shape, dim)


def mod(value, size):
    return lax.rem(value + size, size)


def column(row):
    n = row.shape[1]
    wide = jnp.broadcast_to(row.astype(F32), (n, n))
    return jnp.sum(jnp.where(iota((n, n), 0) == iota((n, n), 1), wide, 0.0), axis=1, keepdims=True)


def hot(row, size):
    return (iota((size, row.shape[1]), 0) == row).astype(F32).astype(BF16)


def kernel(
    feat_hbm, weight_hbm, bias_hbm, degree_hbm, dst_hbm, src_hbm, rows_hbm, count_hbm, target_hbm, cot_hbm,
    act_hbm, gfeat_hbm, gw_hbm, gb_hbm,
    feat_ref, weight_ref, bias_ref, degree_ref, dst_ref, src_ref, rows_ref, count_ref, target_ref, cot_ref,
    act_ref, gfeat_ref, gw_ref, gb_ref,
    xall, gall, acc, own_part, counts_t, psend, precv, gblk, sendtab, loctab, mid, tab,
    w1s, w1r, w2r, w3r, w4r,
    in_sem, out_sem, xs_send, xs_recv, gs_send, gs_recv, p_send, p_recv, q_send, q_recv,
    i1_send, i1_recv, i2_send, i2_recv, w_send, w_recv,
):
    dom = lax.axis_index("dom")
    blk = lax.axis_index("blk")
    c = lax.rem(dom, CN)
    z = lax.rem(lax.div(dom, CN), ZN)
    y = lax.div(dom, CN * ZN)

    def at(yy, zz, cc):
        return (yy * ZN + zz) * CN + cc

    def each(count, body):
        def run(i, carry):
            body(i)
            return carry

        lax.fori_loop(1, count, run, 0)

    barrier = pltpu.get_barrier_semaphore()

    def greet(to_dom, to_blk):
        pl.semaphore_signal(barrier, inc=1, device_id=(to_dom, to_blk), device_id_type=pl.DeviceIdType.MESH)

    def greet_a(i):
        a = mod(blk * CN + c + i, NB * CN)
        greet(at(y, z, lax.rem(a, CN)), lax.div(a, CN))

    def greet_y(i):
        other = mod(y * CN + c + i, YH * CN)
        greet(at(lax.div(other, CN), z, lax.rem(other, CN)), blk)

    for i in range(1, ZN):
        greet(at(y, mod(z + i, ZN), c), blk)
    for i in range(1, YH):
        greet(at(mod(y + i, YH), z, c), blk)
        greet(at(mod(y + i, YH), z, 1 - c), blk)
    each(NB * CN, greet_a)

    incoming = [
        pltpu.make_async_copy(src, dst, in_sem.at[i])
        for i, (src, dst) in enumerate(
            (
                (degree_hbm, degree_ref), (feat_hbm, feat_ref), (count_hbm.at[0], count_ref),
                (rows_hbm.at[0, 0], rows_ref), (target_hbm.at[0, 0], target_ref), (dst_hbm, dst_ref),
                (src_hbm, src_ref), (weight_hbm, weight_ref), (bias_hbm, bias_ref), (cot_hbm, cot_ref),
            )
        )
    ]
    for copy in incoming:
        copy.start()

    outgoing = [
        pltpu.make_async_copy(src, dst, out_sem.at[i])
        for i, (src, dst) in enumerate(
            ((act_ref, act_hbm), (gfeat_ref, gfeat_hbm), (gw_ref, gw_hbm), (gb_ref, gb_hbm))
        )
    ]

    def remote(src, dst, send, recv, to_dom, to_blk):
        return pltpu.make_async_remote_copy(
            src_ref=src, dst_ref=dst, send_sem=send, recv_sem=recv,
            device_id=(to_dom, to_blk), device_id_type=pl.DeviceIdType.MESH,
        )

    def taken(ref, send, recv):
        return remote(ref, ref, send, recv, dom, blk)

    incoming[0].wait()
    incoming[1].wait()
    scale = lax.rsqrt(column(degree_ref[...]))
    xs = (scale * feat_ref[...].astype(F32)).astype(BF16)
    xall[dom] = xs

    pl.semaphore_wait(barrier, (NB * CN - 1) + (ZN - 1) + 2 * (YH - 1))

    def block_copy(buf, send, recv, e, to_dom):
        return remote(buf.at[e], buf.at[e], send, recv.at[e], to_dom, blk)

    def own_sends(buf, send, recv):
        for to_dom in (
            at(y, mod(z + 1, ZN), c), at(y, mod(z - 1, ZN), c),
            at(mod(y - 1, YH), z, c), at(mod(y + 1, YH), z, c), at(mod(y + 2, YH), z, c),
            at(y, z, 1 - c),
        ):
            block_copy(buf, send, recv, dom, to_dom).start()

    def y_block(t):
        return jnp.where(t == 0, 1, jnp.where(t == 1, 3, 2))

    def dy_of(k):
        return jnp.where(k == 0, 0, y_block(k - 1))

    def far_sign(k):
        return jnp.where(k < 2, 1, -1)

    def gather_loop(buf, send, recv, extra, forward):
        def contribution(m):
            pieces = []
            for cc in range(CN):
                e = m * CN + cc
                lanes = iota((1, 2 * HUB), 1)
                mine = jnp.where((lanes < HUB) == forward, loctab[pl.ds(e, 1), :], -1)
                theirs = tab[lax.rem(m, ZN), lax.div(m, ZN) * CN + cc]
                pieces.append(
                    lax.dot_general(hot(mine, ROWS), hot(theirs, ROWS), NT, preferred_element_type=F32).astype(BF16)
                )
            joint = jnp.concatenate(pieces, axis=1)
            return jnp.dot(joint, buf[pl.ds(m * CN, CN)].reshape(CN * ROWS, FIN), preferred_element_type=F32)

        def wait_block(e):
            block_copy(buf, send, recv, e, dom).wait_recv()

        def group(g, carry):
            k = lax.rem(g, 4)
            s = lax.div(g, 4) + 1
            row = mod(y + dy_of(k), YH) * ZN

            @pl.when(g < 4)
            def _():
                wait_block((row + z) * CN + 1 - c)
                acc[...] += contribution(row + z)

            @pl.when(g < 12)
            def _():
                up = row + mod(z - s, ZN)
                down = row + mod(z + s, ZN)
                wait_block(up * CN + 1 - c)
                wait_block(down * CN + 1 - c)
                acc[...] += contribution(up) + contribution(down)

            @pl.when(g >= 12)
            def _():
                m = row + mod(z + 4, ZN)
                wait_block(m * CN + 1 - c)
                acc[...] += contribution(m)

            return carry

        def step(t, low):
            k = lax.rem(t, 4)
            s = lax.div(t, 4) + 1

            @pl.when(t < 3)
            def _():
                e = at(mod(y + y_block(t), YH), z, c)
                wait_block(e)
                block_copy(buf, send, recv, e, at(y, mod(z + 1, ZN), c)).start()
                block_copy(buf, send, recv, e, at(y, mod(z - 1, ZN), c)).start()
                block_copy(buf, send, recv, e, at(y, z, 1 - c)).start()

            @pl.when(t < 16)
            def _():
                for sign in (1, -1):
                    far = far_sign(k) == sign

                    @pl.when((s < 4) | far)
                    def _():
                        e = at(mod(y + dy_of(k), YH), mod(z - sign * s, ZN), c)
                        wait_block(e)

                        @pl.when((s < 3) | ((s == 3) & far))
                        def _():
                            block_copy(buf, send, recv, e, at(y, mod(z + sign, ZN), c)).start()

                        block_copy(buf, send, recv, e, at(y, z, 1 - c)).start()

            extra(t)
            if forward:
                high = jnp.where(t < 5, 0, jnp.minimum(2 * (t - 4), t))
            else:
                high = t
            lax.fori_loop(low, high, group, 0)
            return high

        lax.fori_loop(0, 17, step, 0)
        taken(buf.at[pl.ds(0, YH * ZN * CN - 1)], send, recv.at[0]).wait_send()

    own_sends(xall, xs_send, xs_recv)

    incoming[2].wait()
    incoming[3].wait()
    incoming[4].wait()
    live = iota((HUB, HUB), 1).astype(F32) < column(count_ref[...])
    rows = jnp.where(live, rows_ref[...], ROWS)
    target = target_ref[...]
    joint_tab = jnp.concatenate([rows, target], axis=1)
    loctab[...] = jnp.concatenate([target, rows], axis=1)
    for e in range(YH * ZN * CN):
        sendtab[(e // CN) % ZN, (e // (CN * ZN)) * CN + e % CN] = joint_tab[e : e + 1, :]

    def table_z(i):
        zz = mod(z + i, ZN)
        return remote(sendtab.at[zz], mid.at[z], i1_send, i1_recv, at(y, zz, c), blk)

    def table_yc(i):
        other = mod(y * CN + c + i, YH * CN)
        to_dom = at(lax.div(other, CN), z, lax.rem(other, CN))
        return remote(mid.at[:, other], tab.at[:, y * CN + c], i2_send, i2_recv, to_dom, blk)

    each(ZN, lambda i: table_z(i).start())
    mid[z] = sendtab[z]
    acc[...] = jnp.zeros_like(acc)
    incoming[5].wait()
    incoming[6].wait()

    def part_copy(a):
        return remote(psend.at[a], precv.at[blk], p_send, p_recv, dom, a)

    def forward_extra(t):
        @pl.when(t == 1)
        def _():
            taken(mid.at[pl.ds(0, ZN - 1)], i1_send, i1_recv).wait_recv()
            each(YH * CN, lambda i: table_yc(i).start())
            tab[:, y * CN + c] = mid[:, y * CN + c]

        @pl.when(t < NB)
        def _():
            a = mod(blk + 1 + t, NB)
            dst_hot = hot(dst_ref[a], ROWS)
            src_hot = hot(src_ref[a], ROWS)
            count = lax.dot_general(dst_hot, src_hot, NT, preferred_element_type=F32).astype(BF16)
            count_t = lax.dot_general(src_hot, dst_hot, NT, preferred_element_type=F32).astype(BF16)
            counts_t[a] = count_t
            part = jnp.dot(count, xall[dom], preferred_element_type=F32)

            @pl.when(a != blk)
            def _():
                psend[a] = part.astype(BF16)
                part_copy(a).start()

            @pl.when(a == blk)
            def _():
                own_part[...] = part
                precv[blk] = jnp.zeros((ROWS, FIN), BF16)

        @pl.when(t == 5)
        def _():
            taken(tab.at[pl.ds(0, YH * CN - 1)], i2_send, i2_recv).wait_recv()

        @pl.when(t == 14)
        def _():
            taken(precv.at[pl.ds(0, NB - 1)], p_send, p_recv).wait_recv()
            part = own_part[...]
            for i in range(NB):
                part = part + precv[i].astype(F32)
            acc[...] += part

    gather_loop(xall, xs_send, xs_recv, forward_extra, True)

    for i in (7, 8, 9):
        incoming[i].wait()
    total = acc[...]
    weight = weight_ref[...]
    pre = scale * jnp.dot(total.astype(BF16), weight, preferred_element_type=F32) + bias_ref[...]
    sig = jax.nn.sigmoid(pre)
    grad_pre = cot_ref[...].astype(F32) * sig * (1.0 + pre * (1.0 - sig))
    back = (scale * grad_pre).astype(BF16)
    grad = lax.dot_general(back, weight, NT, preferred_element_type=F32).astype(BF16)
    gall[dom] = grad
    own_sends(gall, gs_send, gs_recv)
    gblk[blk] = grad

    def member_copy(i):
        return remote(gall.at[dom], gblk.at[blk], q_send, q_recv, dom, mod(blk + i, NB))

    each(NB, lambda i: member_copy(i).start())

    act_ref[...] = (pre * sig).astype(BF16)
    outgoing[0].start()
    bias_term = jnp.sum(grad_pre, axis=0, keepdims=True)
    gw = jnp.dot(total.T.astype(BF16), back, preferred_element_type=F32)
    me_a = blk * CN + c
    for a in range(NB * CN):
        w1s[a, 0:8, :] = gw[8 * a : 8 * a + 8, 0:128]
        w1s[a, 8:16, :] = gw[8 * a : 8 * a + 8, 128:256]
        w1s[a, 16:17, :] = bias_term[:, 0:128]
        w1s[a, 17:18, :] = bias_term[:, 128:256]
    w1r[me_a] = w1s[me_a]

    def w1_copy(i):
        a = mod(me_a + i, NB * CN)
        return remote(
            w1s.at[a], w1r.at[me_a], w_send.at[0], w_recv.at[0], at(y, z, lax.rem(a, CN)), lax.div(a, CN)
        )

    def w2_copy(i):
        return remote(w2r.at[y], w2r.at[y], w_send.at[1], w_recv.at[1], at(mod(y + i, YH), z, c), blk)

    def w3_copy(i):
        return remote(w3r.at[z], w3r.at[z], w_send.at[2], w_recv.at[2], at(y, mod(z + i, ZN), c), blk)

    def w4_copy(i):
        a = mod(me_a + i, NB * CN)
        return remote(
            w4r.at[me_a], w4r.at[me_a], w_send.at[3], w_recv.at[3], at(y, z, lax.rem(a, CN)), lax.div(a, CN)
        )

    def others(ref, count, which):
        return taken(ref.at[pl.ds(0, count - 1)], w_send.at[which], w_recv.at[which])

    each(NB * CN, lambda i: w1_copy(i).start())

    acc[...] = jnp.zeros_like(acc)

    def backward_extra(t):
        @pl.when(t == 4)
        def _():
            others(w1r, NB * CN, 0).wait_recv()
            w2r[y] = jnp.sum(w1r[...], axis=0)
            each(YH, lambda i: w2_copy(i).start())

        @pl.when(t == 8)
        def _():
            others(w2r, YH, 1).wait_recv()
            w3r[z] = jnp.sum(w2r[...], axis=0)
            each(ZN, lambda i: w3_copy(i).start())

        @pl.when(t == 12)
        def _():
            others(w3r, ZN, 2).wait_recv()
            w4r[me_a] = jnp.sum(w3r[...], axis=0)
            each(NB * CN, lambda i: w4_copy(i).start())

        @pl.when(t == 14)
        def _():
            taken(gblk.at[pl.ds(0, NB - 1)], q_send, q_recv).wait_recv()
            total_back = acc[...]
            for a in range(NB):
                total_back = total_back + jnp.dot(counts_t[a], gblk[a], preferred_element_type=F32)
            acc[...] = total_back

    gather_loop(gall, gs_send, gs_recv, backward_extra, False)

    gfeat_ref[...] = (scale * acc[...]).astype(BF16)
    outgoing[1].start()
    others(w4r, NB * CN, 3).wait_recv()
    for a in range(NB * CN):
        gw_ref[8 * a : 8 * a + 8, 0:128] = w4r[a, 0:8, :]
        gw_ref[8 * a : 8 * a + 8, 128:256] = w4r[a, 8:16, :]
    gb_ref[...] = w4r[me_a, 16:18, :]
    outgoing[2].start()
    outgoing[3].start()

    taken(mid.at[pl.ds(0, ZN - 1)], i1_send, i1_recv).wait_send()
    taken(tab.at[pl.ds(0, YH * CN - 1)], i2_send, i2_recv).wait_send()
    taken(precv.at[pl.ds(0, NB - 1)], p_send, p_recv).wait_send()
    taken(gblk.at[pl.ds(0, NB - 1)], q_send, q_recv).wait_send()
    others(w1r, NB * CN, 0).wait_send()
    others(w2r, YH, 1).wait_send()
    others(w3r, ZN, 2).wait_send()
    others(w4r, NB * CN, 3).wait_send()
    for copy in outgoing:
        copy.wait()


def write_kernel(act, gfeat, gw, gb, act_out, gfeat_out, gw_out, gb_out, act_v, gfeat_v, gw_v, gb_v, sem):
    through = ((gw, gw_v, gw_out), (act, act_v, act_out), (gfeat, gfeat_v, gfeat_out), (gb, gb_v, gb_out))
    reads = [pltpu.make_async_copy(src, mid, sem.at[i]) for i, (src, mid, dst) in enumerate(through)]
    writes = [pltpu.make_async_copy(mid, dst, sem.at[4 + i]) for i, (src, mid, dst) in enumerate(through)]
    for copy in reads:
        copy.start()
    for read, write in zip(reads, writes):
        read.wait()
        write.start()
    for copy in writes:
        copy.wait()


def per_device(features, weight, out_bias, degree, edge_dst, edge_src, hub_rows, hub_count, hub_target, cotangent):
    nd = YH * ZN * CN
    hbm = pl.BlockSpec(memory_space=pltpu.HBM)
    dma = pltpu.SemaphoreType.DMA
    shapes = (
        jax.ShapeDtypeStruct((ROWS, HID), BF16),
        jax.ShapeDtypeStruct((ROWS, FIN), BF16),
        jax.ShapeDtypeStruct((FIN, HID), F32),
        jax.ShapeDtypeStruct((2, 128), F32),
    )
    results = pl.pallas_call(
        kernel,
        out_shape=shapes,
        in_specs=[hbm] * 10,
        out_specs=(hbm,) * 4,
        scratch_shapes=[
            pltpu.VMEM((ROWS, FIN), BF16),
            pltpu.VMEM((FIN, HID), BF16),
            pltpu.VMEM((1, HID), F32),
            pltpu.VMEM((1, ROWS), jnp.int32),
            pltpu.VMEM((NB, 1, EB), jnp.int32),
            pltpu.VMEM((NB, 1, EB), jnp.int32),
            pltpu.VMEM((HUB, HUB), jnp.int32),
            pltpu.VMEM((1, HUB), jnp.int32),
            pltpu.VMEM((HUB, HUB), jnp.int32),
            pltpu.VMEM((ROWS, HID), BF16),
            pltpu.VMEM((ROWS, HID), BF16),
            pltpu.VMEM((ROWS, FIN), BF16),
            pltpu.VMEM((FIN, HID), F32),
            pltpu.VMEM((2, 128), F32),
            pltpu.VMEM((nd, ROWS, FIN), BF16),
            pltpu.VMEM((nd, ROWS, FIN), BF16),
            pltpu.VMEM((ROWS, FIN), F32),
            pltpu.VMEM((ROWS, FIN), F32),
            pltpu.VMEM((NB, ROWS, ROWS), BF16),
            pltpu.VMEM((NB, ROWS, FIN), BF16),
            pltpu.VMEM((NB, ROWS, FIN), BF16),
            pltpu.VMEM((NB, ROWS, FIN), BF16),
            pltpu.VMEM((ZN, YH * CN, 1, 2 * HUB), jnp.int32),
            pltpu.VMEM((nd, 2 * HUB), jnp.int32),
            pltpu.VMEM((ZN, YH * CN, 1, 2 * HUB), jnp.int32),
            pltpu.VMEM((ZN, YH * CN, 1, 2 * HUB), jnp.int32),
            pltpu.VMEM((NB * CN, 18, 128), F32),
            pltpu.VMEM((NB * CN, 18, 128), F32),
            pltpu.VMEM((YH, 18, 128), F32),
            pltpu.VMEM((ZN, 18, 128), F32),
            pltpu.VMEM((NB * CN, 18, 128), F32),
            dma((10,)), dma((4,)), dma(()), dma((nd,)), dma(()), dma((nd,)),
            dma(()), dma(()), dma(()), dma(()), dma(()), dma(()), dma(()), dma(()), dma((4,)), dma((4,)),
        ],
        compiler_params=pltpu.CompilerParams(
            collective_id=0, has_side_effects=True, vmem_limit_bytes=60 * 1024 * 1024
        ),
    )(
        features, weight, out_bias.reshape(1, HID), degree.reshape(1, ROWS), edge_dst, edge_src,
        hub_rows, hub_count, hub_target, cotangent,
    )
    act, gfeat, gw, gb = pl.pallas_call(
        write_kernel,
        out_shape=shapes,
        in_specs=[hbm] * 4,
        out_specs=(hbm,) * 4,
        scratch_shapes=[pltpu.VMEM(shape.shape, shape.dtype) for shape in shapes] + [dma((8,))],
        compiler_params=pltpu.CompilerParams(vmem_limit_bytes=60 * 1024 * 1024),
    )(*results)
    return act, gfeat, gw, gb.reshape(HID)


def solution(mesh):
    return jax.shard_map(
        per_device,
        mesh=mesh,
        in_specs=(
            P(("dom", "blk"), None),
            P(),
            P(),
            P(("dom", "blk")),
            P("dom", "blk", None),
            P("dom", "blk", None),
            P("dom", "blk", None, None),
            P("dom", "blk", None),
            P("dom", "blk", None, None),
            P(("dom", "blk"), None),
        ),
        out_specs=(P(("dom", "blk"), None), P(("dom", "blk"), None), P(), P()),
        check_vma=False,
    )
```

```python
import functools

import jax
import jax.numpy as jnp
from jax import lax
from jax.experimental import pallas as pl
from jax.experimental.pallas import tpu as pltpu
from jax.sharding import PartitionSpec as P

F32 = jnp.float32
BF16 = jnp.bfloat16
NT = (((1,), (1,)), ((), ()))
YH, ZN, CN, NB = 4, 8, 2, 8
ROWS, FIN, HID, HUB, EB = 128, 128, 256, 64, 384


def iota(shape, dim):
    return lax.broadcasted_iota(jnp.int32, shape, dim)


def mod(value, size):
    return lax.rem(value + size, size)


def column(row):
    n = row.shape[1]
    wide = jnp.broadcast_to(row.astype(F32), (n, n))
    return jnp.sum(jnp.where(iota((n, n), 0) == iota((n, n), 1), wide, 0.0), axis=1, keepdims=True)


def hot(row, size):
    return (iota((size, row.shape[1]), 0) == row).astype(F32).astype(BF16)


def kernel(
    feat_hbm, weight_hbm, bias_hbm, degree_hbm, dst_hbm, src_hbm, rows_hbm, count_hbm, target_hbm, cot_hbm,
    act_hbm, gfeat_hbm, gw_hbm, gb_hbm,
    feat_ref, weight_ref, bias_ref, degree_ref, dst_ref, src_ref, rows_ref, count_ref, target_ref, cot_ref,
    act_ref, gfeat_ref, gw_ref, gb_ref,
    xrow, grow, hacc, hout, hin, bout, bin_, own_part, counts_t, psend, precv, gblk, sendtab, loctab, mid, ya, mf, mb,
    w1s, w1r, w2r, w3r, w4r,
    in_sem, out_sem, xs_send, xs_recv, gs_send, gs_recv, h_send, h_recv, p_send, p_recv, q_send, q_recv,
    i_send, i_recv, w_send, w_recv,
):
    dom = lax.axis_index("dom")
    blk = lax.axis_index("blk")
    c = lax.rem(dom, CN)
    z = lax.rem(lax.div(dom, CN), ZN)
    y = lax.div(dom, CN * ZN)

    def at(yy, zz, cc):
        return (yy * ZN + zz) * CN + cc

    def each(count, body):
        def run(i, carry):
            body(i)
            return carry

        lax.fori_loop(1, count, run, 0)

    barrier = pltpu.get_barrier_semaphore()

    def greet(to_dom, to_blk):
        pl.semaphore_signal(barrier, inc=1, device_id=(to_dom, to_blk), device_id_type=pl.DeviceIdType.MESH)

    def greet_a(i):
        a = mod(blk * CN + c + i, NB * CN)
        greet(at(y, z, lax.rem(a, CN)), lax.div(a, CN))

    for i in range(1, ZN):
        greet(at(y, mod(z + i, ZN), c), blk)
    for i in range(1, YH):
        greet(at(mod(y + i, YH), z, c), blk)
    each(NB * CN, greet_a)

    incoming = [
        pltpu.make_async_copy(src, dst, in_sem.at[i])
        for i, (src, dst) in enumerate(
            (
                (degree_hbm, degree_ref), (feat_hbm, feat_ref), (count_hbm.at[0], count_ref),
                (rows_hbm.at[0, 0], rows_ref), (target_hbm.at[0, 0], target_ref), (dst_hbm, dst_ref),
                (src_hbm, src_ref), (weight_hbm, weight_ref), (bias_hbm, bias_ref), (cot_hbm, cot_ref),
            )
        )
    ]
    for copy in incoming:
        copy.start()

    outgoing = [
        pltpu.make_async_copy(src, dst, out_sem.at[i])
        for i, (src, dst) in enumerate(
            ((act_ref, act_hbm), (gfeat_ref, gfeat_hbm), (gw_ref, gw_hbm), (gb_ref, gb_hbm))
        )
    ]

    def remote(src, dst, send, recv, to_dom, to_blk):
        return pltpu.make_async_remote_copy(
            src_ref=src, dst_ref=dst, send_sem=send, recv_sem=recv,
            device_id=(to_dom, to_blk), device_id_type=pl.DeviceIdType.MESH,
        )

    def taken(ref, send, recv):
        return remote(ref, ref, send, recv, dom, blk)

    incoming[0].wait()
    incoming[1].wait()
    scale = lax.rsqrt(column(degree_ref[...]))
    xrow[z, c] = (scale * feat_ref[...].astype(F32)).astype(BF16)

    for i in (2, 3, 4):
        incoming[i].wait()
    live = iota((HUB, HUB), 1).astype(F32) < column(count_ref[...])
    rows = jnp.where(live, rows_ref[...], ROWS)
    target = target_ref[...]
    joint_tab = jnp.concatenate([rows, target], axis=1)
    loctab[...] = jnp.concatenate([target, rows], axis=1).reshape(YH, ZN * CN, 2 * HUB)
    for e in range(YH * ZN * CN):
        sendtab[(e // CN) % ZN, (e // (CN * ZN)) * CN + e % CN] = joint_tab[e : e + 1, :]

    def table_z(i):
        zz = mod(z + i, ZN)
        return remote(sendtab.at[zz], mid.at[c, z], i_send.at[0], i_recv.at[0], at(y, zz, c), blk)

    def table_y(i):
        yy = mod(y + i, YH)
        return remote(loctab.at[yy], ya.at[y], i_send.at[1], i_recv.at[1], at(yy, z, c), blk)

    table_relay = remote(mid.at[c], mid.at[c], i_send.at[2], i_recv.at[2], at(y, z, 1 - c), blk)

    def block_copy(buf, send, recv, zz, cc, to_dom, kind=0):
        return remote(buf.at[zz, cc], buf.at[zz, cc], send.at[kind], recv.at[zz, cc], to_dom, blk)

    def distance(j):
        half = lax.div(j + 1, 2)
        return jnp.where(lax.rem(j, 2) == 1, half, ZN - half)

    def line_sends(buf, send, recv):
        for i in (4, 3, 5, 2, 6, 1, 7):
            block_copy(buf, send, recv, z, c, at(y, mod(z + i, ZN), c)).start()
        block_copy(buf, send, recv, z, c, at(y, z, 1 - c), 1).start()

    def build(counts, zz, forward):
        keep = (iota((1, 2 * HUB), 1) < HUB) == forward
        for yy in range(YH):
            for cc in range(CN):
                mine = jnp.where(keep, ya[yy, pl.ds(zz * CN + cc, 1), :], -1)
                theirs = mid[cc, zz, yy * CN + c]
                counts[zz, yy, :, cc * ROWS : (cc + 1) * ROWS] = lax.dot_general(
                    hot(mine, ROWS), hot(theirs, ROWS), NT, preferred_element_type=F32
                ).astype(BF16)

    def line_loop(buf, send, recv, counts, prepare):
        hacc[...] = jnp.zeros_like(hacc)

        def step(j, carry):
            zz = mod(z + distance(j), ZN)
            prepare(j, zz)

            @pl.when(j < ZN - 1)
            def _():
                after = mod(z + distance(j + 1), ZN)
                block_copy(buf, send, recv, after, c, dom).wait_recv()
                block_copy(buf, send, recv, after, c, at(y, z, 1 - c), 1).start()

            block_copy(buf, send, recv, zz, 1 - c, dom).wait_recv()
            part = jnp.dot(
                counts[zz].reshape(YH * ROWS, CN * ROWS), buf[zz].reshape(CN * ROWS, FIN), preferred_element_type=F32
            )
            hacc[...] += part.reshape(YH, ROWS, FIN)
            return carry

        lax.fori_loop(0, ZN, step, 0)

    def sum_sends(out, inn, which):
        for i in (2, 1, 3):
            yy = mod(y + i, YH)
            out[yy] = hacc[yy].astype(BF16)
            remote(out.at[yy], inn.at[y], h_send.at[which], h_recv.at[which], at(yy, z, c), blk).start()
        inn[y] = jnp.zeros((ROWS, FIN), BF16)

    def sums(inn, which):
        return taken(inn.at[pl.ds(0, YH - 1)], h_send.at[which], h_recv.at[which])

    pl.semaphore_wait(barrier, (NB * CN - 1) + (ZN - 1) + (YH - 1))

    for i in (4, 3, 5, 2, 6, 1, 7):
        table_z(i).start()
    line_sends(xrow, xs_send, xs_recv)
    for i in (2, 1, 3):
        table_y(i).start()
    mid[c, z] = sendtab[z]
    ya[y] = loctab[y]

    incoming[5].wait()
    incoming[6].wait()

    def part_copy(a):
        return remote(psend.at[a], precv.at[blk], p_send, p_recv, dom, a)

    def local_part(i, carry):
        a = mod(blk + 1 + i, NB)
        dst_hot = hot(dst_ref[a], ROWS)
        src_hot = hot(src_ref[a], ROWS)
        count = lax.dot_general(dst_hot, src_hot, NT, preferred_element_type=F32).astype(BF16)
        counts_t[a] = lax.dot_general(src_hot, dst_hot, NT, preferred_element_type=F32).astype(BF16)
        part = jnp.dot(count, xrow[z, c], preferred_element_type=F32)

        @pl.when(i < NB - 1)
        def _():
            psend[a] = part.astype(BF16)
            part_copy(a).start()

        @pl.when(i == NB - 1)
        def _():
            own_part[...] = part
            precv[a] = jnp.zeros((ROWS, FIN), BF16)

        return carry

    lax.fori_loop(0, NB, local_part, 0)

    taken(mid.at[c, pl.ds(0, ZN - 1)], i_send.at[0], i_recv.at[0]).wait_recv()
    table_relay.start()
    taken(ya.at[pl.ds(0, YH - 1)], i_send.at[1], i_recv.at[1]).wait_recv()
    remote(mid.at[1 - c], mid.at[1 - c], i_send.at[2], i_recv.at[2], dom, blk).wait_recv()

    line_loop(xrow, xs_send, xs_recv, mf, lambda j, zz: build(mf, zz, True))
    sum_sends(hout, hin, 0)

    def build_back(zz, carry):
        build(mb, zz, False)
        return carry

    lax.fori_loop(0, ZN, build_back, 0)
    total = hacc[y] + own_part[...]
    taken(precv.at[pl.ds(0, NB - 1)], p_send, p_recv).wait_recv()
    for i in range(NB):
        total = total + precv[i].astype(F32)
    sums(hin, 0).wait_recv()
    for i in range(YH):
        total = total + hin[i].astype(F32)

    for i in (7, 8, 9):
        incoming[i].wait()
    weight = weight_ref[...]
    pre = scale * jnp.dot(total.astype(BF16), weight, preferred_element_type=F32) + bias_ref[...]
    sig = jax.nn.sigmoid(pre)
    grad_pre = cot_ref[...].astype(F32) * sig * (1.0 + pre * (1.0 - sig))
    back = (scale * grad_pre).astype(BF16)
    grad = lax.dot_general(back, weight, NT, preferred_element_type=F32).astype(BF16)
    grow[z, c] = grad
    line_sends(grow, gs_send, gs_recv)
    gblk[blk] = grad

    def member_copy(i):
        return remote(grow.at[z, c], gblk.at[blk], q_send, q_recv, dom, mod(blk + i, NB))

    bias_term = jnp.sum(grad_pre, axis=0, keepdims=True)
    gw = jnp.dot(total.T.astype(BF16), back, preferred_element_type=F32)
    me_a = blk * CN + c
    for a in range(NB * CN):
        w1s[a, 0:8, :] = gw[8 * a : 8 * a + 8, 0:128]
        w1s[a, 8:16, :] = gw[8 * a : 8 * a + 8, 128:256]
        w1s[a, 16:17, :] = bias_term[:, 0:128]
        w1s[a, 17:18, :] = bias_term[:, 128:256]
    w1r[me_a] = w1s[me_a]

    def w1_copy(i):
        a = mod(me_a + i, NB * CN)
        return remote(
            w1s.at[a], w1r.at[me_a], w_send.at[0], w_recv.at[0], at(y, z, lax.rem(a, CN)), lax.div(a, CN)
        )

    def w2_copy(i):
        return remote(w2r.at[y], w2r.at[y], w_send.at[1], w_recv.at[1], at(mod(y + i, YH), z, c), blk)

    def w3_copy(i):
        return remote(w3r.at[z], w3r.at[z], w_send.at[2], w_recv.at[2], at(y, mod(z + i, ZN), c), blk)

    def w4_copy(i):
        a = mod(me_a + i, NB * CN)
        return remote(
            w4r.at[me_a], w4r.at[me_a], w_send.at[3], w_recv.at[3], at(y, z, lax.rem(a, CN)), lax.div(a, CN)
        )

    def others(ref, count, which):
        return taken(ref.at[pl.ds(0, count - 1)], w_send.at[which], w_recv.at[which])

    each(NB * CN, lambda i: w1_copy(i).start())
    each(NB, lambda i: member_copy(i).start())
    act_ref[...] = (pre * sig).astype(BF16)
    outgoing[0].start()

    def backward_extra(j, zz):
        @pl.when(j == 4)
        def _():
            others(w1r, NB * CN, 0).wait_recv()
            w2r[y] = jnp.sum(w1r[...], axis=0)
            each(YH, lambda i: w2_copy(i).start())

    line_loop(grow, gs_send, gs_recv, mb, backward_extra)
    sum_sends(bout, bin_, 1)

    taken(gblk.at[pl.ds(0, NB - 1)], q_send, q_recv).wait_recv()
    total_back = hacc[y]
    for a in range(NB):
        total_back = total_back + jnp.dot(counts_t[a], gblk[a], preferred_element_type=F32)

    others(w2r, YH, 1).wait_recv()
    w3r[z] = jnp.sum(w2r[...], axis=0)
    each(ZN, lambda i: w3_copy(i).start())

    sums(bin_, 1).wait_recv()
    for i in range(YH):
        total_back = total_back + bin_[i].astype(F32)
    gfeat_ref[...] = (scale * total_back).astype(BF16)
    outgoing[1].start()

    others(w3r, ZN, 2).wait_recv()
    w4r[me_a] = jnp.sum(w3r[...], axis=0)
    each(NB * CN, lambda i: w4_copy(i).start())

    others(w4r, NB * CN, 3).wait_recv()
    for a in range(NB * CN):
        gw_ref[8 * a : 8 * a + 8, 0:128] = w4r[a, 0:8, :]
        gw_ref[8 * a : 8 * a + 8, 128:256] = w4r[a, 8:16, :]
    gb_ref[...] = w4r[me_a, 16:18, :]
    outgoing[2].start()
    outgoing[3].start()

    for send, recv in ((xs_send, xs_recv), (gs_send, gs_recv)):
        taken(psend.at[pl.ds(0, ZN - 1)], send.at[0], recv.at[0, 0]).wait_send()
        taken(psend, send.at[1], recv.at[0, 0]).wait_send()
    taken(mid.at[c, pl.ds(0, ZN - 1)], i_send.at[0], i_recv.at[0]).wait_send()
    taken(ya.at[pl.ds(0, YH - 1)], i_send.at[1], i_recv.at[1]).wait_send()
    table_relay.wait_send()
    sums(hin, 0).wait_send()
    sums(bin_, 1).wait_send()
    taken(precv.at[pl.ds(0, NB - 1)], p_send, p_recv).wait_send()
    taken(gblk.at[pl.ds(0, NB - 1)], q_send, q_recv).wait_send()
    others(w1r, NB * CN, 0).wait_send()
    others(w2r, YH, 1).wait_send()
    others(w3r, ZN, 2).wait_send()
    others(w4r, NB * CN, 3).wait_send()
    for copy in outgoing:
        copy.wait()


def write_kernel(act, gfeat, gw, gb, act_out, gfeat_out, gw_out, gb_out, act_v, gfeat_v, gw_v, gb_v, sem):
    through = ((gw, gw_v, gw_out), (act, act_v, act_out), (gfeat, gfeat_v, gfeat_out), (gb, gb_v, gb_out))
    reads = [pltpu.make_async_copy(src, mid, sem.at[i]) for i, (src, mid, dst) in enumerate(through)]
    writes = [pltpu.make_async_copy(mid, dst, sem.at[4 + i]) for i, (src, mid, dst) in enumerate(through)]
    for copy in reads:
        copy.start()
    for read, write in zip(reads, writes):
        read.wait()
        write.start()
    for copy in writes:
        copy.wait()


def per_device(features, weight, out_bias, degree, edge_dst, edge_src, hub_rows, hub_count, hub_target, cotangent):
    hbm = pl.BlockSpec(memory_space=pltpu.HBM)
    dma = pltpu.SemaphoreType.DMA
    shapes = (
        jax.ShapeDtypeStruct((ROWS, HID), BF16),
        jax.ShapeDtypeStruct((ROWS, FIN), BF16),
        jax.ShapeDtypeStruct((FIN, HID), F32),
        jax.ShapeDtypeStruct((2, 128), F32),
    )
    results = pl.pallas_call(
        kernel,
        out_shape=shapes,
        in_specs=[hbm] * 10,
        out_specs=(hbm,) * 4,
        scratch_shapes=[
            pltpu.VMEM((ROWS, FIN), BF16),
            pltpu.VMEM((FIN, HID), BF16),
            pltpu.VMEM((1, HID), F32),
            pltpu.VMEM((1, ROWS), jnp.int32),
            pltpu.VMEM((NB, 1, EB), jnp.int32),
            pltpu.VMEM((NB, 1, EB), jnp.int32),
            pltpu.VMEM((HUB, HUB), jnp.int32),
            pltpu.VMEM((1, HUB), jnp.int32),
            pltpu.VMEM((HUB, HUB), jnp.int32),
            pltpu.VMEM((ROWS, HID), BF16),
            pltpu.VMEM((ROWS, HID), BF16),
            pltpu.VMEM((ROWS, FIN), BF16),
            pltpu.VMEM((FIN, HID), F32),
            pltpu.VMEM((2, 128), F32),
            pltpu.VMEM((ZN, CN, ROWS, FIN), BF16),
            pltpu.VMEM((ZN, CN, ROWS, FIN), BF16),
            pltpu.VMEM((YH, ROWS, FIN), F32),
            pltpu.VMEM((YH, ROWS, FIN), BF16),
            pltpu.VMEM((YH, ROWS, FIN), BF16),
            pltpu.VMEM((YH, ROWS, FIN), BF16),
            pltpu.VMEM((YH, ROWS, FIN), BF16),
            pltpu.VMEM((ROWS, FIN), F32),
            pltpu.VMEM((NB, ROWS, ROWS), BF16),
            pltpu.VMEM((NB, ROWS, FIN), BF16),
            pltpu.VMEM((NB, ROWS, FIN), BF16),
            pltpu.VMEM((NB, ROWS, FIN), BF16),
            pltpu.VMEM((ZN, YH * CN, 1, 2 * HUB), jnp.int32),
            pltpu.VMEM((YH, ZN * CN, 2 * HUB), jnp.int32),
            pltpu.VMEM((CN, ZN, YH * CN, 1, 2 * HUB), jnp.int32),
            pltpu.VMEM((YH, ZN * CN, 2 * HUB), jnp.int32),
            pltpu.VMEM((ZN, YH, ROWS, CN * ROWS), BF16),
            pltpu.VMEM((ZN, YH, ROWS, CN * ROWS), BF16),
            pltpu.VMEM((NB * CN, 18, 128), F32),
            pltpu.VMEM((NB * CN, 18, 128), F32),
            pltpu.VMEM((YH, 18, 128), F32),
            pltpu.VMEM((ZN, 18, 128), F32),
            pltpu.VMEM((NB * CN, 18, 128), F32),
            dma((10,)), dma((4,)), dma((2,)), dma((ZN, CN)), dma((2,)), dma((ZN, CN)),
            dma((2,)), dma((2,)), dma(()), dma(()), dma(()), dma(()), dma((3,)), dma((3,)), dma((4,)), dma((4,)),
        ],
        compiler_params=pltpu.CompilerParams(
            collective_id=0, has_side_effects=True, vmem_limit_bytes=60 * 1024 * 1024
        ),
    )(
        features, weight, out_bias.reshape(1, HID), degree.reshape(1, ROWS), edge_dst, edge_src,
        hub_rows, hub_count, hub_target, cotangent,
    )
    act, gfeat, gw, gb = pl.pallas_call(
        write_kernel,
        out_shape=shapes,
        in_specs=[hbm] * 4,
        out_specs=(hbm,) * 4,
        scratch_shapes=[pltpu.VMEM(shape.shape, shape.dtype) for shape in shapes] + [dma((8,))],
        compiler_params=pltpu.CompilerParams(vmem_limit_bytes=60 * 1024 * 1024),
    )(*results)
    return act, gfeat, gw, gb.reshape(HID)


def solution(mesh):
    return jax.shard_map(
        per_device,
        mesh=mesh,
        in_specs=(
            P(("dom", "blk"), None),
            P(),
            P(),
            P(("dom", "blk")),
            P("dom", "blk", None),
            P("dom", "blk", None),
            P("dom", "blk", None, None),
            P("dom", "blk", None),
            P("dom", "blk", None, None),
            P(("dom", "blk"), None),
        ),
        out_specs=(P(("dom", "blk"), None), P(("dom", "blk"), None), P(), P()),
        check_vma=False,
    )
```

```python
import functools

import jax
import jax.numpy as jnp
from jax import lax
from jax.experimental import pallas as pl
from jax.experimental.pallas import tpu as pltpu
from jax.sharding import PartitionSpec as P

F32 = jnp.float32
BF16 = jnp.bfloat16
NT = (((1,), (1,)), ((), ()))
YH, ZN, CN, NB = 4, 8, 2, 8
ROWS, FIN, HID, HUB, EB = 128, 128, 256, 64, 384


def iota(shape, dim):
    return lax.broadcasted_iota(jnp.int32, shape, dim)


def mod(value, size):
    return lax.rem(value + size, size)


def column(row):
    n = row.shape[1]
    wide = jnp.broadcast_to(row.astype(F32), (n, n))
    return jnp.sum(jnp.where(iota((n, n), 0) == iota((n, n), 1), wide, 0.0), axis=1, keepdims=True)


def hot(row, size):
    return (iota((size, row.shape[1]), 0) == row).astype(F32).astype(BF16)


def kernel(
    feat_hbm, weight_hbm, bias_hbm, degree_hbm, dst_hbm, src_hbm, rows_hbm, count_hbm, target_hbm, cot_hbm,
    act_hbm, gfeat_hbm, gw_hbm, gb_hbm,
    feat_ref, weight_ref, bias_ref, degree_ref, dst_ref, src_ref, rows_ref, count_ref, target_ref, cot_ref,
    act_ref, gfeat_ref, gw_ref, gb_ref,
    xrow, grow, hacc, hout, hin, bout, bin_, own_part, counts_t, psend, precv, gblk, sendtab, loctab, mid, ya, mf, mb,
    w1s, w1r, w2r, w3r,
    in_sem, out_sem, xs_send, xs_recv, gs_send, gs_recv, h_send, h_recv, p_send, p_recv, q_send, q_recv,
    i_send, i_recv, w_send, w_recv,
):
    dom = lax.axis_index("dom")
    blk = lax.axis_index("blk")
    c = lax.rem(dom, CN)
    z = lax.rem(lax.div(dom, CN), ZN)
    y = lax.div(dom, CN * ZN)

    def at(yy, zz, cc):
        return (yy * ZN + zz) * CN + cc

    def each(count, body):
        def run(i, carry):
            body(i)
            return carry

        lax.fori_loop(1, count, run, 0)

    barrier = pltpu.get_barrier_semaphore()

    def greet(to_dom, to_blk):
        pl.semaphore_signal(barrier, inc=1, device_id=(to_dom, to_blk), device_id_type=pl.DeviceIdType.MESH)

    for i in range(1, ZN):
        greet(at(y, mod(z + i, ZN), c), blk)
    for i in range(1, YH):
        greet(at(mod(y + i, YH), z, c), blk)
    greet(at(y, z, 1 - c), blk)
    for i in range(1, NB):
        greet(dom, mod(blk + i, NB))

    incoming = [
        pltpu.make_async_copy(src, dst, in_sem.at[i])
        for i, (src, dst) in enumerate(
            (
                (degree_hbm, degree_ref), (feat_hbm, feat_ref), (count_hbm.at[0], count_ref),
                (rows_hbm.at[0, 0], rows_ref), (target_hbm.at[0, 0], target_ref), (dst_hbm, dst_ref),
                (src_hbm, src_ref), (weight_hbm, weight_ref), (bias_hbm, bias_ref), (cot_hbm, cot_ref),
            )
        )
    ]
    for copy in incoming:
        copy.start()

    outgoing = [
        pltpu.make_async_copy(src, dst, out_sem.at[i])
        for i, (src, dst) in enumerate(
            ((act_ref, act_hbm), (gfeat_ref, gfeat_hbm), (gw_ref, gw_hbm), (gb_ref, gb_hbm))
        )
    ]

    def remote(src, dst, send, recv, to_dom, to_blk):
        return pltpu.make_async_remote_copy(
            src_ref=src, dst_ref=dst, send_sem=send, recv_sem=recv,
            device_id=(to_dom, to_blk), device_id_type=pl.DeviceIdType.MESH,
        )

    def taken(ref, send, recv):
        return remote(ref, ref, send, recv, dom, blk)

    incoming[0].wait()
    incoming[1].wait()
    scale = lax.rsqrt(column(degree_ref[...]))
    xrow[z, c] = (scale * feat_ref[...].astype(F32)).astype(BF16)

    for i in (2, 3, 4):
        incoming[i].wait()
    live = iota((HUB, HUB), 1).astype(F32) < column(count_ref[...])
    rows = jnp.where(live, rows_ref[...], ROWS)
    target = target_ref[...]
    joint_tab = jnp.concatenate([rows, target], axis=1)
    loctab[...] = jnp.concatenate([target, rows], axis=1).reshape(YH, ZN * CN, 2 * HUB)
    for e in range(YH * ZN * CN):
        sendtab[(e // CN) % ZN, (e // (CN * ZN)) * CN + e % CN] = joint_tab[e : e + 1, :]

    def table_z(i):
        zz = mod(z + i, ZN)
        return remote(sendtab.at[zz], mid.at[c, z], i_send.at[0], i_recv.at[0], at(y, zz, c), blk)

    def table_y(i):
        yy = mod(y + i, YH)
        return remote(loctab.at[yy], ya.at[y], i_send.at[1], i_recv.at[1], at(yy, z, c), blk)

    table_relay = remote(mid.at[c], mid.at[c], i_send.at[2], i_recv.at[2], at(y, z, 1 - c), blk)

    def block_copy(buf, send, recv, zz, cc, to_dom, kind=0):
        return remote(buf.at[zz, cc], buf.at[zz, cc], send.at[kind], recv.at[zz, cc], to_dom, blk)

    def distance(j):
        half = lax.div(j + 1, 2)
        return jnp.where(lax.rem(j, 2) == 1, half, ZN - half)

    def line_sends(buf, send, recv):
        for i in (1, 7, 2, 6, 3, 5, 4):
            block_copy(buf, send, recv, z, c, at(y, mod(z + i, ZN), c)).start()
        block_copy(buf, send, recv, z, c, at(y, z, 1 - c), 1).start()

    def build(counts, zz, forward):
        keep = (iota((1, 2 * HUB), 1) < HUB) == forward
        for yy in range(YH):
            for cc in range(CN):
                mine = jnp.where(keep, ya[yy, pl.ds(zz * CN + cc, 1), :], -1)
                theirs = mid[cc, zz, yy * CN + c]
                counts[zz, yy, :, cc * ROWS : (cc + 1) * ROWS] = lax.dot_general(
                    hot(mine, ROWS), hot(theirs, ROWS), NT, preferred_element_type=F32
                ).astype(BF16)

    def line_loop(buf, send, recv, counts, prepare):
        hacc[...] = jnp.zeros_like(hacc)

        def step(j, carry):
            zz = mod(z + distance(j), ZN)
            prepare(j, zz)

            @pl.when(j < ZN - 1)
            def _():
                after = mod(z + distance(j + 1), ZN)
                block_copy(buf, send, recv, after, c, dom).wait_recv()
                block_copy(buf, send, recv, after, c, at(y, z, 1 - c), 1).start()

            block_copy(buf, send, recv, zz, 1 - c, dom).wait_recv()
            part = jnp.dot(
                counts[zz].reshape(YH * ROWS, CN * ROWS), buf[zz].reshape(CN * ROWS, FIN), preferred_element_type=F32
            )
            hacc[...] += part.reshape(YH, ROWS, FIN)
            return carry

        lax.fori_loop(0, ZN, step, 0)

    def sum_sends(out, inn, which):
        for i in (2, 1, 3):
            yy = mod(y + i, YH)
            out[yy] = hacc[yy].astype(BF16)
            remote(out.at[yy], inn.at[y], h_send.at[which], h_recv.at[which], at(yy, z, c), blk).start()
        inn[y] = jnp.zeros((ROWS, FIN), BF16)

    def sums(inn, which):
        return taken(inn.at[pl.ds(0, YH - 1)], h_send.at[which], h_recv.at[which])

    pl.semaphore_wait(barrier, (NB - 1) + (ZN - 1) + (YH - 1) + 1)

    for i in (4, 3, 5, 2, 6, 1, 7):
        table_z(i).start()
    line_sends(xrow, xs_send, xs_recv)
    for i in (2, 1, 3):
        table_y(i).start()
    mid[c, z] = sendtab[z]
    ya[y] = loctab[y]

    incoming[5].wait()
    incoming[6].wait()

    def part_copy(a):
        return remote(psend.at[a], precv.at[blk], p_send, p_recv, dom, a)

    def local_part(i, carry):
        a = mod(blk + 1 + i, NB)
        dst_hot = hot(dst_ref[a], ROWS)
        src_hot = hot(src_ref[a], ROWS)
        count = lax.dot_general(dst_hot, src_hot, NT, preferred_element_type=F32).astype(BF16)
        counts_t[a] = lax.dot_general(src_hot, dst_hot, NT, preferred_element_type=F32).astype(BF16)
        part = jnp.dot(count, xrow[z, c], preferred_element_type=F32)

        @pl.when(i < NB - 1)
        def _():
            psend[a] = part.astype(BF16)
            part_copy(a).start()

        @pl.when(i == NB - 1)
        def _():
            own_part[...] = part
            precv[a] = jnp.zeros((ROWS, FIN), BF16)

        return carry

    lax.fori_loop(0, NB, local_part, 0)

    taken(mid.at[c, pl.ds(0, ZN - 1)], i_send.at[0], i_recv.at[0]).wait_recv()
    table_relay.start()
    taken(ya.at[pl.ds(0, YH - 1)], i_send.at[1], i_recv.at[1]).wait_recv()
    remote(mid.at[1 - c], mid.at[1 - c], i_send.at[2], i_recv.at[2], dom, blk).wait_recv()

    line_loop(xrow, xs_send, xs_recv, mf, lambda j, zz: build(mf, zz, True))
    taken(precv.at[pl.ds(0, NB - 1)], p_send, p_recv).wait_recv()
    sum_sends(hout, hin, 0)

    def build_back(zz, carry):
        build(mb, zz, False)
        return carry

    lax.fori_loop(0, ZN, build_back, 0)
    total = hacc[y] + own_part[...]
    for i in range(NB):
        total = total + precv[i].astype(F32)
    sums(hin, 0).wait_recv()
    for i in range(YH):
        total = total + hin[i].astype(F32)

    for i in (7, 8, 9):
        incoming[i].wait()
    weight = weight_ref[...]
    pre = scale * jnp.dot(total.astype(BF16), weight, preferred_element_type=F32) + bias_ref[...]
    sig = jax.nn.sigmoid(pre)
    grad_pre = cot_ref[...].astype(F32) * sig * (1.0 + pre * (1.0 - sig))
    back = (scale * grad_pre).astype(BF16)
    grad = lax.dot_general(back, weight, NT, preferred_element_type=F32).astype(BF16)
    bias_term = jnp.sum(grad_pre, axis=0, keepdims=True)
    gw = jnp.dot(total.T.astype(BF16), back, preferred_element_type=F32)
    grow[z, c] = grad
    line_sends(grow, gs_send, gs_recv)
    me_a = blk * YH + y
    me_b = z * CN + c
    for a in range(NB * YH):
        g, h = a // 2, a % 2
        w1s[a, 0:8, :] = gw[8 * g : 8 * g + 8, 128 * h : 128 * h + 128]
        w1s[a, 8:9, :] = bias_term[:, 0:128]
        w1s[a, 9:10, :] = bias_term[:, 128:256]
    w1r[me_a] = w1s[me_a]

    def peer(i):
        a = mod(me_a + i, NB * YH)
        return a, at(lax.rem(a, YH), z, c), lax.div(a, YH)

    def w1_copy(i):
        a, to_dom, to_blk = peer(i)
        return remote(w1s.at[a], w1r.at[me_a], w_send.at[0], w_recv.at[0], to_dom, to_blk)

    def w2_copy(i):
        b = mod(me_b + i, ZN * CN)
        return remote(w2r.at[me_b], w2r.at[me_b], w_send.at[1], w_recv.at[1], y * (ZN * CN) + b, blk)

    def w3_copy(i):
        a, to_dom, to_blk = peer(i)
        return remote(w3r.at[me_a], w3r.at[me_a], w_send.at[2], w_recv.at[2], to_dom, to_blk)

    gblk[blk] = grad

    def member_copy(i):
        return remote(grow.at[z, c], gblk.at[blk], q_send, q_recv, dom, mod(blk + i, NB))

    def others(ref, count, which):
        return taken(ref.at[pl.ds(0, count - 1)], w_send.at[which], w_recv.at[which])

    each(NB * YH, lambda i: w1_copy(i).start())
    each(NB, lambda i: member_copy(i).start())
    act_ref[...] = (pre * sig).astype(BF16)
    outgoing[0].start()

    def backward_extra(j, zz):
        @pl.when(j == 6)
        def _():
            others(w1r, NB * YH, 0).wait_recv()
            w2r[me_b] = jnp.sum(w1r[...], axis=0)
            each(ZN * CN, lambda i: w2_copy(i).start())

    line_loop(grow, gs_send, gs_recv, mb, backward_extra)
    sum_sends(bout, bin_, 1)

    taken(gblk.at[pl.ds(0, NB - 1)], q_send, q_recv).wait_recv()
    total_back = hacc[y]
    for a in range(NB):
        total_back = total_back + jnp.dot(counts_t[a], gblk[a], preferred_element_type=F32)

    others(w2r, ZN * CN, 1).wait_recv()
    w3r[me_a] = jnp.sum(w2r[...], axis=0)
    each(NB * YH, lambda i: w3_copy(i).start())

    sums(bin_, 1).wait_recv()
    for i in range(YH):
        total_back = total_back + bin_[i].astype(F32)
    gfeat_ref[...] = (scale * total_back).astype(BF16)
    outgoing[1].start()

    others(w3r, NB * YH, 2).wait_recv()
    for a in range(NB * YH):
        g, h = a // 2, a % 2
        gw_ref[8 * g : 8 * g + 8, 128 * h : 128 * h + 128] = w3r[a, 0:8, :]
    gb_ref[...] = w3r[me_a, 8:10, :]
    outgoing[2].start()
    outgoing[3].start()

    for send, recv in ((xs_send, xs_recv), (gs_send, gs_recv)):
        taken(psend.at[pl.ds(0, ZN - 1)], send.at[0], recv.at[0, 0]).wait_send()
        taken(psend, send.at[1], recv.at[0, 0]).wait_send()
    taken(mid.at[c, pl.ds(0, ZN - 1)], i_send.at[0], i_recv.at[0]).wait_send()
    taken(ya.at[pl.ds(0, YH - 1)], i_send.at[1], i_recv.at[1]).wait_send()
    table_relay.wait_send()
    sums(hin, 0).wait_send()
    sums(bin_, 1).wait_send()
    taken(precv.at[pl.ds(0, NB - 1)], p_send, p_recv).wait_send()
    taken(gblk.at[pl.ds(0, NB - 1)], q_send, q_recv).wait_send()
    others(w1r, NB * YH, 0).wait_send()
    others(w2r, ZN * CN, 1).wait_send()
    others(w3r, NB * YH, 2).wait_send()
    for copy in outgoing:
        copy.wait()


def write_kernel(act, gfeat, gw, gb, act_out, gfeat_out, gw_out, gb_out, act_v, gfeat_v, gw_v, gb_v, sem):
    through = ((gw, gw_v, gw_out), (act, act_v, act_out), (gfeat, gfeat_v, gfeat_out), (gb, gb_v, gb_out))
    reads = [pltpu.make_async_copy(src, mid, sem.at[i]) for i, (src, mid, dst) in enumerate(through)]
    writes = [pltpu.make_async_copy(mid, dst, sem.at[4 + i]) for i, (src, mid, dst) in enumerate(through)]
    for copy in reads:
        copy.start()
    for read, write in zip(reads, writes):
        read.wait()
        write.start()
    for copy in writes:
        copy.wait()


def per_device(features, weight, out_bias, degree, edge_dst, edge_src, hub_rows, hub_count, hub_target, cotangent):
    hbm = pl.BlockSpec(memory_space=pltpu.HBM)
    dma = pltpu.SemaphoreType.DMA
    shapes = (
        jax.ShapeDtypeStruct((ROWS, HID), BF16),
        jax.ShapeDtypeStruct((ROWS, FIN), BF16),
        jax.ShapeDtypeStruct((FIN, HID), F32),
        jax.ShapeDtypeStruct((2, 128), F32),
    )
    results = pl.pallas_call(
        kernel,
        out_shape=shapes,
        in_specs=[hbm] * 10,
        out_specs=(hbm,) * 4,
        scratch_shapes=[
            pltpu.VMEM((ROWS, FIN), BF16),
            pltpu.VMEM((FIN, HID), BF16),
            pltpu.VMEM((1, HID), F32),
            pltpu.VMEM((1, ROWS), jnp.int32),
            pltpu.VMEM((NB, 1, EB), jnp.int32),
            pltpu.VMEM((NB, 1, EB), jnp.int32),
            pltpu.VMEM((HUB, HUB), jnp.int32),
            pltpu.VMEM((1, HUB), jnp.int32),
            pltpu.VMEM((HUB, HUB), jnp.int32),
            pltpu.VMEM((ROWS, HID), BF16),
            pltpu.VMEM((ROWS, HID), BF16),
            pltpu.VMEM((ROWS, FIN), BF16),
            pltpu.VMEM((FIN, HID), F32),
            pltpu.VMEM((2, 128), F32),
            pltpu.VMEM((ZN, CN, ROWS, FIN), BF16),
            pltpu.VMEM((ZN, CN, ROWS, FIN), BF16),
            pltpu.VMEM((YH, ROWS, FIN), F32),
            pltpu.VMEM((YH, ROWS, FIN), BF16),
            pltpu.VMEM((YH, ROWS, FIN), BF16),
            pltpu.VMEM((YH, ROWS, FIN), BF16),
            pltpu.VMEM((YH, ROWS, FIN), BF16),
            pltpu.VMEM((ROWS, FIN), F32),
            pltpu.VMEM((NB, ROWS, ROWS), BF16),
            pltpu.VMEM((NB, ROWS, FIN), BF16),
            pltpu.VMEM((NB, ROWS, FIN), BF16),
            pltpu.VMEM((NB, ROWS, FIN), BF16),
            pltpu.VMEM((ZN, YH * CN, 1, 2 * HUB), jnp.int32),
            pltpu.VMEM((YH, ZN * CN, 2 * HUB), jnp.int32),
            pltpu.VMEM((CN, ZN, YH * CN, 1, 2 * HUB), jnp.int32),
            pltpu.VMEM((YH, ZN * CN, 2 * HUB), jnp.int32),
            pltpu.VMEM((ZN, YH, ROWS, CN * ROWS), BF16),
            pltpu.VMEM((ZN, YH, ROWS, CN * ROWS), BF16),
            pltpu.VMEM((NB * YH, 10, 128), F32),
            pltpu.VMEM((NB * YH, 10, 128), F32),
            pltpu.VMEM((ZN * CN, 10, 128), F32),
            pltpu.VMEM((NB * YH, 10, 128), F32),
            dma((10,)), dma((4,)), dma((2,)), dma((ZN, CN)), dma((2,)), dma((ZN, CN)),
            dma((2,)), dma((2,)), dma(()), dma(()), dma(()), dma(()), dma((3,)), dma((3,)), dma((3,)), dma((3,)),
        ],
        compiler_params=pltpu.CompilerParams(
            collective_id=0, has_side_effects=True, vmem_limit_bytes=60 * 1024 * 1024
        ),
    )(
        features, weight, out_bias.reshape(1, HID), degree.reshape(1, ROWS), edge_dst, edge_src,
        hub_rows, hub_count, hub_target, cotangent,
    )
    act, gfeat, gw, gb = pl.pallas_call(
        write_kernel,
        out_shape=shapes,
        in_specs=[hbm] * 4,
        out_specs=(hbm,) * 4,
        scratch_shapes=[pltpu.VMEM(shape.shape, shape.dtype) for shape in shapes] + [dma((8,))],
        compiler_params=pltpu.CompilerParams(vmem_limit_bytes=60 * 1024 * 1024),
    )(*results)
    return act, gfeat, gw, gb.reshape(HID)


def solution(mesh):
    return jax.shard_map(
        per_device,
        mesh=mesh,
        in_specs=(
            P(("dom", "blk"), None),
            P(),
            P(),
            P(("dom", "blk")),
            P("dom", "blk", None),
            P("dom", "blk", None),
            P("dom", "blk", None, None),
            P("dom", "blk", None),
            P("dom", "blk", None, None),
            P(("dom", "blk"), None),
        ),
        out_specs=(P(("dom", "blk"), None), P(("dom", "blk"), None), P(), P()),
        check_vma=False,
    )
```

```python
import functools

import jax
import jax.numpy as jnp
from jax import lax
from jax.experimental import pallas as pl
from jax.experimental.pallas import tpu as pltpu
from jax.sharding import PartitionSpec as P

F32 = jnp.float32
BF16 = jnp.bfloat16
NT = (((1,), (1,)), ((), ()))
YH, ZN, CN, NB = 4, 8, 2, 8
ROWS, FIN, HID, HUB, EB = 128, 128, 256, 64, 384


def ring(step, size):
    return min(step, size - step)


FAR_AY = sorted(
    ((dx, flip, dy) for dx in range(4) for flip in range(2) for dy in range(YH) if dx or flip or dy),
    key=lambda step: -(ring(step[0], 4) + step[1] + 2 * ring(step[2], YH)),
)
FAR_ZC = sorted(((dz, flip) for dz in range(ZN) for flip in range(CN) if dz or flip), key=lambda step: -ring(step[0], ZN))


def iota(shape, dim):
    return lax.broadcasted_iota(jnp.int32, shape, dim)


def mod(value, size):
    return lax.rem(value + size, size)


def column(row):
    n = row.shape[1]
    wide = jnp.broadcast_to(row.astype(F32), (n, n))
    return jnp.sum(jnp.where(iota((n, n), 0) == iota((n, n), 1), wide, 0.0), axis=1, keepdims=True)


def hot(row, size):
    return (iota((size, row.shape[1]), 0) == row).astype(F32).astype(BF16)


def kernel(
    feat_hbm, weight_hbm, bias_hbm, degree_hbm, dst_hbm, src_hbm, rows_hbm, count_hbm, target_hbm, cot_hbm,
    act_hbm, gfeat_hbm, gw_hbm, gb_hbm,
    feat_ref, weight_ref, bias_ref, degree_ref, dst_ref, src_ref, rows_ref, count_ref, target_ref, cot_ref,
    act_ref, gfeat_ref, gb_ref,
    xrow, grow, hacc, hout, hin, bout, bin_, own_part, counts_t, psend, precv, gblk, sendtab, loctab, mid, ya, mf, mb,
    w1s, w1r, w2r, w3r,
    in_sem, out_sem, xs_send, xs_recv, gs_send, gs_recv, h_send, h_recv, p_send, p_recv, q_send, q_recv,
    i_send, i_recv, w_send, w_recv,
):
    dom = lax.axis_index("dom")
    blk = lax.axis_index("blk")
    c = lax.rem(dom, CN)
    z = lax.rem(lax.div(dom, CN), ZN)
    y = lax.div(dom, CN * ZN)

    def at(yy, zz, cc):
        return (yy * ZN + zz) * CN + cc

    def each(count, body):
        def run(i, carry):
            body(i)
            return carry

        lax.fori_loop(1, count, run, 0)

    barrier = pltpu.get_barrier_semaphore()

    def greet(to_dom, to_blk):
        pl.semaphore_signal(barrier, inc=1, device_id=(to_dom, to_blk), device_id_type=pl.DeviceIdType.MESH)

    for i in range(1, ZN):
        greet(at(y, mod(z + i, ZN), c), blk)
    for i in range(1, YH):
        greet(at(mod(y + i, YH), z, c), blk)
    greet(at(y, z, 1 - c), blk)
    for i in range(1, NB):
        greet(dom, mod(blk + i, NB))

    incoming = [
        pltpu.make_async_copy(src, dst, in_sem.at[i])
        for i, (src, dst) in enumerate(
            (
                (degree_hbm, degree_ref), (feat_hbm, feat_ref), (count_hbm.at[0], count_ref),
                (rows_hbm.at[0, 0], rows_ref), (target_hbm.at[0, 0], target_ref), (dst_hbm, dst_ref),
                (src_hbm, src_ref), (weight_hbm, weight_ref), (bias_hbm, bias_ref), (cot_hbm, cot_ref),
            )
        )
    ]
    for copy in incoming:
        copy.start()

    outgoing = [
        pltpu.make_async_copy(src, dst, out_sem.at[3 if i == 2 else i])
        for i, (src, dst) in enumerate(
            ((act_ref, act_hbm), (gfeat_ref, gfeat_hbm), (gb_ref, gb_hbm))
        )
    ]

    def remote(src, dst, send, recv, to_dom, to_blk):
        return pltpu.make_async_remote_copy(
            src_ref=src, dst_ref=dst, send_sem=send, recv_sem=recv,
            device_id=(to_dom, to_blk), device_id_type=pl.DeviceIdType.MESH,
        )

    def taken(ref, send, recv):
        return remote(ref, ref, send, recv, dom, blk)

    incoming[0].wait()
    incoming[1].wait()
    scale = lax.rsqrt(column(degree_ref[...]))
    xrow[z, c] = (scale * feat_ref[...].astype(F32)).astype(BF16)

    for i in (2, 3, 4):
        incoming[i].wait()
    live = iota((HUB, HUB), 1).astype(F32) < column(count_ref[...])
    rows = jnp.where(live, rows_ref[...], ROWS)
    target = target_ref[...]
    joint_tab = jnp.concatenate([rows, target], axis=1)
    loctab[...] = jnp.concatenate([target, rows], axis=1).reshape(YH, ZN * CN, 2 * HUB)
    for e in range(YH * ZN * CN):
        sendtab[(e // CN) % ZN, (e // (CN * ZN)) * CN + e % CN] = joint_tab[e : e + 1, :]

    def table_z(i):
        zz = mod(z + i, ZN)
        return remote(sendtab.at[zz], mid.at[c, z], i_send.at[0], i_recv.at[0], at(y, zz, c), blk)

    def table_y(i):
        yy = mod(y + i, YH)
        return remote(loctab.at[yy], ya.at[y], i_send.at[1], i_recv.at[1], at(yy, z, c), blk)

    table_relay = remote(mid.at[c], mid.at[c], i_send.at[2], i_recv.at[2], at(y, z, 1 - c), blk)

    def block_copy(buf, send, recv, zz, cc, to_dom, kind=0):
        return remote(buf.at[zz, cc], buf.at[zz, cc], send.at[kind], recv.at[zz, cc], to_dom, blk)

    def distance(j):
        half = lax.div(j + 1, 2)
        return jnp.where(lax.rem(j, 2) == 1, half, ZN - half)

    def line_sends(buf, send, recv):
        for i in (1, 7, 2, 6, 3, 5, 4):
            block_copy(buf, send, recv, z, c, at(y, mod(z + i, ZN), c)).start()
        block_copy(buf, send, recv, z, c, at(y, z, 1 - c), 1).start()

    def build(counts, zz, forward):
        keep = (iota((1, 2 * HUB), 1) < HUB) == forward
        for yy in range(YH):
            for cc in range(CN):
                mine = jnp.where(keep, ya[yy, pl.ds(zz * CN + cc, 1), :], -1)
                theirs = mid[cc, zz, yy * CN + c]
                counts[zz, yy, :, cc * ROWS : (cc + 1) * ROWS] = lax.dot_general(
                    hot(mine, ROWS), hot(theirs, ROWS), NT, preferred_element_type=F32
                ).astype(BF16)

    def line_loop(buf, send, recv, counts, prepare):
        hacc[...] = jnp.zeros_like(hacc)

        def step(j, carry):
            zz = mod(z + distance(j), ZN)
            prepare(j, zz)

            @pl.when(j < ZN - 1)
            def _():
                after = mod(z + distance(j + 1), ZN)
                block_copy(buf, send, recv, after, c, dom).wait_recv()
                block_copy(buf, send, recv, after, c, at(y, z, 1 - c), 1).start()

            block_copy(buf, send, recv, zz, 1 - c, dom).wait_recv()
            part = jnp.dot(
                counts[zz].reshape(YH * ROWS, CN * ROWS), buf[zz].reshape(CN * ROWS, FIN), preferred_element_type=F32
            )
            hacc[...] += part.reshape(YH, ROWS, FIN)
            return carry

        lax.fori_loop(0, ZN, step, 0)

    def sum_sends(out, inn, which):
        for i in (2, 1, 3):
            yy = mod(y + i, YH)
            out[yy] = hacc[yy].astype(BF16)
            remote(out.at[yy], inn.at[y], h_send.at[which], h_recv.at[which], at(yy, z, c), blk).start()
        inn[y] = jnp.zeros((ROWS, FIN), BF16)

    def sums(inn, which):
        return taken(inn.at[pl.ds(0, YH - 1)], h_send.at[which], h_recv.at[which])

    pl.semaphore_wait(barrier, (NB - 1) + (ZN - 1) + (YH - 1) + 1)

    for i in (4, 3, 5, 2, 6, 1, 7):
        table_z(i).start()
    line_sends(xrow, xs_send, xs_recv)
    for i in (2, 1, 3):
        table_y(i).start()
    mid[c, z] = sendtab[z]
    ya[y] = loctab[y]

    incoming[5].wait()
    incoming[6].wait()

    def part_copy(a):
        return remote(psend.at[a], precv.at[blk], p_send, p_recv, dom, a)

    def local_part(i, carry):
        a = mod(blk + 1 + i, NB)
        dst_hot = hot(dst_ref[a], ROWS)
        src_hot = hot(src_ref[a], ROWS)
        count = lax.dot_general(dst_hot, src_hot, NT, preferred_element_type=F32).astype(BF16)
        counts_t[a] = lax.dot_general(src_hot, dst_hot, NT, preferred_element_type=F32).astype(BF16)
        part = jnp.dot(count, xrow[z, c], preferred_element_type=F32)

        @pl.when(i < NB - 1)
        def _():
            psend[a] = part.astype(BF16)
            part_copy(a).start()

        @pl.when(i == NB - 1)
        def _():
            own_part[...] = part
            precv[a] = jnp.zeros((ROWS, FIN), BF16)

        return carry

    lax.fori_loop(0, NB, local_part, 0)

    taken(mid.at[c, pl.ds(0, ZN - 1)], i_send.at[0], i_recv.at[0]).wait_recv()
    table_relay.start()
    taken(ya.at[pl.ds(0, YH - 1)], i_send.at[1], i_recv.at[1]).wait_recv()
    remote(mid.at[1 - c], mid.at[1 - c], i_send.at[2], i_recv.at[2], dom, blk).wait_recv()

    line_loop(xrow, xs_send, xs_recv, mf, lambda j, zz: build(mf, zz, True))
    taken(precv.at[pl.ds(0, NB - 1)], p_send, p_recv).wait_recv()
    sum_sends(hout, hin, 0)

    def build_back(zz, carry):
        build(mb, zz, False)
        return carry

    lax.fori_loop(0, ZN, build_back, 0)
    total = hacc[y] + own_part[...]
    for i in range(NB):
        total = total + precv[i].astype(F32)
    sums(hin, 0).wait_recv()
    for i in range(YH):
        total = total + hin[i].astype(F32)

    for i in (7, 8, 9):
        incoming[i].wait()
    weight = weight_ref[...]
    pre = scale * jnp.dot(total.astype(BF16), weight, preferred_element_type=F32) + bias_ref[...]
    sig = jax.nn.sigmoid(pre)
    grad_pre = cot_ref[...].astype(F32) * sig * (1.0 + pre * (1.0 - sig))
    back = (scale * grad_pre).astype(BF16)
    grad = lax.dot_general(back, weight, NT, preferred_element_type=F32).astype(BF16)
    bias_term = jnp.sum(grad_pre, axis=0, keepdims=True)
    gw = jnp.dot(total.T.astype(BF16), back, preferred_element_type=F32)
    grow[z, c] = grad
    line_sends(grow, gs_send, gs_recv)
    me_a = blk * YH + y
    me_b = z * CN + c
    for a in range(NB * YH):
        g, h = a // 2, a % 2
        w1s[a, 0:8, :] = gw[8 * g : 8 * g + 8, 128 * h : 128 * h + 128]
        w1s[a, 8:9, :] = bias_term[:, 0:128]
        w1s[a, 9:10, :] = bias_term[:, 128:256]
    w1r[me_a] = w1s[me_a]

    def peer(step):
        dx, flip, dy = step
        to_blk = mod(lax.div(blk, 2) + dx, 4) * 2 + (1 - lax.rem(blk, 2) if flip else lax.rem(blk, 2))
        yy = mod(y + dy, YH)
        return to_blk * YH + yy, at(yy, z, c), to_blk

    gw_piece = gw_hbm.at[pl.ds(pl.multiple_of(me_a // 2 * 8, 8), 8), pl.ds(pl.multiple_of(me_a % 2 * 128, 128), 128)]
    own_piece = pltpu.make_async_copy(w3r.at[me_a], gw_piece, out_sem.at[2])

    def w1_copy(i):
        a, to_dom, to_blk = peer(i)
        return remote(w1s.at[a], w1r.at[me_a], w_send.at[0], w_recv.at[0], to_dom, to_blk)

    def w2_copy(i):
        dz, flip = i
        to_dom = at(y, mod(z + dz, ZN), 1 - c if flip else c)
        return remote(w2r.at[me_b], w2r.at[me_b], w_send.at[1], w_recv.at[1], to_dom, blk)

    def w3_copy(i):
        a, to_dom, to_blk = peer(i)
        return remote(w3r.at[me_a], gw_piece, w_send.at[2], w_recv.at[2], to_dom, to_blk)

    gblk[blk] = grad

    def member_copy(i):
        return remote(grow.at[z, c], gblk.at[blk], q_send, q_recv, dom, mod(blk + i, NB))

    def others(ref, count, which):
        return taken(ref.at[pl.ds(0, count - 1)], w_send.at[which], w_recv.at[which])

    for step in FAR_AY:
        w1_copy(step).start()
    each(NB, lambda i: member_copy(i).start())
    act_ref[...] = (pre * sig).astype(BF16)
    outgoing[0].start()

    def backward_extra(j, zz):
        @pl.when(j == 5)
        def _():
            others(w1r, NB * YH, 0).wait_recv()
            w2r[me_b] = jnp.sum(w1r[...], axis=0)
            for step in FAR_ZC:
                w2_copy(step).start()

    line_loop(grow, gs_send, gs_recv, mb, backward_extra)
    sum_sends(bout, bin_, 1)

    others(w2r, ZN * CN, 1).wait_recv()
    summed = jnp.sum(w2r[...], axis=0)
    w3r[me_a] = summed[0:8]
    for step in FAR_AY:
        w3_copy(step).start()
    own_piece.start()
    gb_ref[...] = summed[8:10]
    outgoing[2].start()

    taken(gblk.at[pl.ds(0, NB - 1)], q_send, q_recv).wait_recv()
    total_back = hacc[y]
    for a in range(NB):
        total_back = total_back + jnp.dot(counts_t[a], gblk[a], preferred_element_type=F32)

    sums(bin_, 1).wait_recv()
    for i in range(YH):
        total_back = total_back + bin_[i].astype(F32)
    gfeat_ref[...] = (scale * total_back).astype(BF16)
    outgoing[1].start()

    others(w3r, NB * YH, 2).wait_recv()
    for send, recv in ((xs_send, xs_recv), (gs_send, gs_recv)):
        taken(psend.at[pl.ds(0, ZN - 1)], send.at[0], recv.at[0, 0]).wait_send()
        taken(psend, send.at[1], recv.at[0, 0]).wait_send()
    taken(mid.at[c, pl.ds(0, ZN - 1)], i_send.at[0], i_recv.at[0]).wait_send()
    taken(ya.at[pl.ds(0, YH - 1)], i_send.at[1], i_recv.at[1]).wait_send()
    table_relay.wait_send()
    sums(hin, 0).wait_send()
    sums(bin_, 1).wait_send()
    taken(precv.at[pl.ds(0, NB - 1)], p_send, p_recv).wait_send()
    taken(gblk.at[pl.ds(0, NB - 1)], q_send, q_recv).wait_send()
    others(w1r, NB * YH, 0).wait_send()
    others(w2r, ZN * CN, 1).wait_send()
    others(w3r, NB * YH, 2).wait_send()
    own_piece.wait()
    for copy in outgoing:
        copy.wait()


def write_kernel(act, gfeat, gw, gb, act_out, gfeat_out, gw_out, gb_out, act_v, gfeat_v, gw_v, gb_v, sem):
    through = ((gw, gw_v, gw_out), (act, act_v, act_out), (gfeat, gfeat_v, gfeat_out), (gb, gb_v, gb_out))
    reads = [pltpu.make_async_copy(src, mid, sem.at[i]) for i, (src, mid, dst) in enumerate(through)]
    writes = [pltpu.make_async_copy(mid, dst, sem.at[4 + i]) for i, (src, mid, dst) in enumerate(through)]
    for copy in reads:
        copy.start()
    for read, write in zip(reads, writes):
        read.wait()
        write.start()
    for copy in writes:
        copy.wait()


def per_device(features, weight, out_bias, degree, edge_dst, edge_src, hub_rows, hub_count, hub_target, cotangent):
    hbm = pl.BlockSpec(memory_space=pltpu.HBM)
    dma = pltpu.SemaphoreType.DMA
    shapes = (
        jax.ShapeDtypeStruct((ROWS, HID), BF16),
        jax.ShapeDtypeStruct((ROWS, FIN), BF16),
        jax.ShapeDtypeStruct((FIN, HID), F32),
        jax.ShapeDtypeStruct((2, 128), F32),
    )
    results = pl.pallas_call(
        kernel,
        out_shape=shapes,
        in_specs=[hbm] * 10,
        out_specs=(hbm,) * 4,
        scratch_shapes=[
            pltpu.VMEM((ROWS, FIN), BF16),
            pltpu.VMEM((FIN, HID), BF16),
            pltpu.VMEM((1, HID), F32),
            pltpu.VMEM((1, ROWS), jnp.int32),
            pltpu.VMEM((NB, 1, EB), jnp.int32),
            pltpu.VMEM((NB, 1, EB), jnp.int32),
            pltpu.VMEM((HUB, HUB), jnp.int32),
            pltpu.VMEM((1, HUB), jnp.int32),
            pltpu.VMEM((HUB, HUB), jnp.int32),
            pltpu.VMEM((ROWS, HID), BF16),
            pltpu.VMEM((ROWS, HID), BF16),
            pltpu.VMEM((ROWS, FIN), BF16),
            pltpu.VMEM((2, 128), F32),
            pltpu.VMEM((ZN, CN, ROWS, FIN), BF16),
            pltpu.VMEM((ZN, CN, ROWS, FIN), BF16),
            pltpu.VMEM((YH, ROWS, FIN), F32),
            pltpu.VMEM((YH, ROWS, FIN), BF16),
            pltpu.VMEM((YH, ROWS, FIN), BF16),
            pltpu.VMEM((YH, ROWS, FIN), BF16),
            pltpu.VMEM((YH, ROWS, FIN), BF16),
            pltpu.VMEM((ROWS, FIN), F32),
            pltpu.VMEM((NB, ROWS, ROWS), BF16),
            pltpu.VMEM((NB, ROWS, FIN), BF16),
            pltpu.VMEM((NB, ROWS, FIN), BF16),
            pltpu.VMEM((NB, ROWS, FIN), BF16),
            pltpu.VMEM((ZN, YH * CN, 1, 2 * HUB), jnp.int32),
            pltpu.VMEM((YH, ZN * CN, 2 * HUB), jnp.int32),
            pltpu.VMEM((CN, ZN, YH * CN, 1, 2 * HUB), jnp.int32),
            pltpu.VMEM((YH, ZN * CN, 2 * HUB), jnp.int32),
            pltpu.VMEM((ZN, YH, ROWS, CN * ROWS), BF16),
            pltpu.VMEM((ZN, YH, ROWS, CN * ROWS), BF16),
            pltpu.VMEM((NB * YH, 10, 128), F32),
            pltpu.VMEM((NB * YH, 10, 128), F32),
            pltpu.VMEM((ZN * CN, 10, 128), F32),
            pltpu.VMEM((NB * YH, 8, 128), F32),
            dma((10,)), dma((4,)), dma((2,)), dma((ZN, CN)), dma((2,)), dma((ZN, CN)),
            dma((2,)), dma((2,)), dma(()), dma(()), dma(()), dma(()), dma((3,)), dma((3,)), dma((3,)), dma((3,)),
        ],
        compiler_params=pltpu.CompilerParams(
            collective_id=0, has_side_effects=True, vmem_limit_bytes=60 * 1024 * 1024
        ),
    )(
        features, weight, out_bias.reshape(1, HID), degree.reshape(1, ROWS), edge_dst, edge_src,
        hub_rows, hub_count, hub_target, cotangent,
    )
    act, gfeat, gw, gb = pl.pallas_call(
        write_kernel,
        out_shape=shapes,
        in_specs=[hbm] * 4,
        out_specs=(hbm,) * 4,
        scratch_shapes=[pltpu.VMEM(shape.shape, shape.dtype) for shape in shapes] + [dma((8,))],
        compiler_params=pltpu.CompilerParams(vmem_limit_bytes=60 * 1024 * 1024),
    )(*results)
    return act, gfeat, gw, gb.reshape(HID)


def solution(mesh):
    return jax.shard_map(
        per_device,
        mesh=mesh,
        in_specs=(
            P(("dom", "blk"), None),
            P(),
            P(),
            P(("dom", "blk")),
            P("dom", "blk", None),
            P("dom", "blk", None),
            P("dom", "blk", None, None),
            P("dom", "blk", None),
            P("dom", "blk", None, None),
            P(("dom", "blk"), None),
        ),
        out_specs=(P(("dom", "blk"), None), P(("dom", "blk"), None), P(), P()),
        check_vma=False,
    )
```

```python
import functools

import jax
import jax.numpy as jnp
from jax import lax
from jax.experimental import pallas as pl
from jax.experimental.pallas import tpu as pltpu
from jax.sharding import PartitionSpec as P

F32 = jnp.float32
BF16 = jnp.bfloat16
NT = (((1,), (1,)), ((), ()))
YH, ZN, CN, NB = 4, 8, 2, 8
ROWS, FIN, HID, HUB, EB = 128, 128, 256, 64, 384


def ring(step, size):
    return min(step, size - step)


FAR_A = sorted(
    ((dx, flip, cross) for dx in range(4) for flip in range(2) for cross in range(CN) if dx or flip or cross),
    key=lambda step: -(ring(step[0], 4) + step[1]),
)
FAR_B = sorted(
    ((dy, dz) for dy in range(YH) for dz in range(ZN) if dy or dz),
    key=lambda step: -(2 * ring(step[0], YH) + ring(step[1], ZN)),
)


def iota(shape, dim):
    return lax.broadcasted_iota(jnp.int32, shape, dim)


def mod(value, size):
    return lax.rem(value + size, size)


def column(row):
    n = row.shape[1]
    wide = jnp.broadcast_to(row.astype(F32), (n, n))
    return jnp.sum(jnp.where(iota((n, n), 0) == iota((n, n), 1), wide, 0.0), axis=1, keepdims=True)


def hot(row, size):
    return (iota((size, row.shape[1]), 0) == row).astype(F32).astype(BF16)


def kernel(
    feat_hbm, weight_hbm, bias_hbm, degree_hbm, dst_hbm, src_hbm, rows_hbm, count_hbm, target_hbm, cot_hbm,
    act_hbm, gfeat_hbm, gw_hbm, gb_hbm,
    feat_ref, weight_ref, bias_ref, degree_ref, dst_ref, src_ref, rows_ref, count_ref, target_ref, cot_ref,
    act_ref, gfeat_ref, gb_ref,
    xrow, grow, hacc, hout, hin, bout, bin_, own_part, counts_t, psend, precv, gblk, sendtab, loctab, mid, ya, mf, mb,
    w1s, w1r, w2r, w2b, w3r,
    in_sem, out_sem, xs_send, xs_recv, gs_send, gs_recv, h_send, h_recv, p_send, p_recv, q_send, q_recv,
    i_send, i_recv, w_send, w_recv,
):
    dom = lax.axis_index("dom")
    blk = lax.axis_index("blk")
    c = lax.rem(dom, CN)
    z = lax.rem(lax.div(dom, CN), ZN)
    y = lax.div(dom, CN * ZN)

    def at(yy, zz, cc):
        return (yy * ZN + zz) * CN + cc

    def each(count, body):
        def run(i, carry):
            body(i)
            return carry

        lax.fori_loop(1, count, run, 0)

    barrier = pltpu.get_barrier_semaphore()

    def greet(to_dom, to_blk):
        pl.semaphore_signal(barrier, inc=1, device_id=(to_dom, to_blk), device_id_type=pl.DeviceIdType.MESH)

    for i in range(1, ZN):
        greet(at(y, mod(z + i, ZN), c), blk)
    for i in range(1, YH):
        greet(at(mod(y + i, YH), z, c), blk)
    for i in range(1, NB * CN):
        a = mod(blk * CN + c + i, NB * CN)
        greet(at(y, z, lax.rem(a, CN)), lax.div(a, CN))

    incoming = [
        pltpu.make_async_copy(src, dst, in_sem.at[i])
        for i, (src, dst) in enumerate(
            (
                (degree_hbm, degree_ref), (feat_hbm, feat_ref), (count_hbm.at[0], count_ref),
                (rows_hbm.at[0, 0], rows_ref), (target_hbm.at[0, 0], target_ref), (dst_hbm, dst_ref),
                (src_hbm, src_ref), (weight_hbm, weight_ref), (bias_hbm, bias_ref), (cot_hbm, cot_ref),
            )
        )
    ]
    for copy in incoming:
        copy.start()

    outgoing = [
        pltpu.make_async_copy(src, dst, out_sem.at[3 if i == 2 else i])
        for i, (src, dst) in enumerate(
            ((act_ref, act_hbm), (gfeat_ref, gfeat_hbm), (gb_ref, gb_hbm))
        )
    ]

    def remote(src, dst, send, recv, to_dom, to_blk):
        return pltpu.make_async_remote_copy(
            src_ref=src, dst_ref=dst, send_sem=send, recv_sem=recv,
            device_id=(to_dom, to_blk), device_id_type=pl.DeviceIdType.MESH,
        )

    def taken(ref, send, recv):
        return remote(ref, ref, send, recv, dom, blk)

    incoming[0].wait()
    incoming[1].wait()
    scale = lax.rsqrt(column(degree_ref[...]))
    xrow[z, c] = (scale * feat_ref[...].astype(F32)).astype(BF16)

    for i in (2, 3, 4):
        incoming[i].wait()
    live = iota((HUB, HUB), 1).astype(F32) < column(count_ref[...])
    rows = jnp.where(live, rows_ref[...], ROWS)
    target = target_ref[...]
    joint_tab = jnp.concatenate([rows, target], axis=1)
    loctab[...] = jnp.concatenate([target, rows], axis=1).reshape(YH, ZN * CN, 2 * HUB)
    for e in range(YH * ZN * CN):
        sendtab[(e // CN) % ZN, (e // (CN * ZN)) * CN + e % CN] = joint_tab[e : e + 1, :]

    def table_z(i):
        zz = mod(z + i, ZN)
        return remote(sendtab.at[zz], mid.at[c, z], i_send.at[0], i_recv.at[0], at(y, zz, c), blk)

    def table_y(i):
        yy = mod(y + i, YH)
        return remote(loctab.at[yy], ya.at[y], i_send.at[1], i_recv.at[1], at(yy, z, c), blk)

    table_relay = remote(mid.at[c], mid.at[c], i_send.at[2], i_recv.at[2], at(y, z, 1 - c), blk)

    def block_copy(buf, send, recv, zz, cc, to_dom, kind=0):
        return remote(buf.at[zz, cc], buf.at[zz, cc], send.at[kind], recv.at[zz, cc], to_dom, blk)

    def distance(j):
        half = lax.div(j + 1, 2)
        return jnp.where(lax.rem(j, 2) == 1, half, ZN - half)

    def line_sends(buf, send, recv):
        for i in (1, 7, 2, 6, 3, 5, 4):
            block_copy(buf, send, recv, z, c, at(y, mod(z + i, ZN), c)).start()
        block_copy(buf, send, recv, z, c, at(y, z, 1 - c), 1).start()

    def build(counts, zz, forward):
        keep = (iota((1, 2 * HUB), 1) < HUB) == forward
        for yy in range(YH):
            for cc in range(CN):
                mine = jnp.where(keep, ya[yy, pl.ds(zz * CN + cc, 1), :], -1)
                theirs = mid[cc, zz, yy * CN + c]
                counts[zz, yy, :, cc * ROWS : (cc + 1) * ROWS] = lax.dot_general(
                    hot(mine, ROWS), hot(theirs, ROWS), NT, preferred_element_type=F32
                ).astype(BF16)

    def line_loop(buf, send, recv, counts, prepare):
        hacc[...] = jnp.zeros_like(hacc)

        def step(j, carry):
            zz = mod(z + distance(j), ZN)
            prepare(j, zz)

            @pl.when(j < ZN - 1)
            def _():
                after = mod(z + distance(j + 1), ZN)
                block_copy(buf, send, recv, after, c, dom).wait_recv()
                block_copy(buf, send, recv, after, c, at(y, z, 1 - c), 1).start()

            block_copy(buf, send, recv, zz, 1 - c, dom).wait_recv()
            part = jnp.dot(
                counts[zz].reshape(YH * ROWS, CN * ROWS), buf[zz].reshape(CN * ROWS, FIN), preferred_element_type=F32
            )
            hacc[...] += part.reshape(YH, ROWS, FIN)
            return carry

        lax.fori_loop(0, ZN, step, 0)

    def sum_sends(out, inn, which):
        for i in (2, 1, 3):
            yy = mod(y + i, YH)
            out[yy] = hacc[yy].astype(BF16)
            remote(out.at[yy], inn.at[y], h_send.at[which], h_recv.at[which], at(yy, z, c), blk).start()
        inn[y] = jnp.zeros((ROWS, FIN), BF16)

    def sums(inn, which):
        return taken(inn.at[pl.ds(0, YH - 1)], h_send.at[which], h_recv.at[which])

    pl.semaphore_wait(barrier, (NB * CN - 1) + (ZN - 1) + (YH - 1))

    for i in (4, 3, 5, 2, 6, 1, 7):
        table_z(i).start()
    line_sends(xrow, xs_send, xs_recv)
    for i in (2, 1, 3):
        table_y(i).start()
    mid[c, z] = sendtab[z]
    ya[y] = loctab[y]

    incoming[5].wait()
    incoming[6].wait()

    def part_copy(a):
        return remote(psend.at[a], precv.at[blk], p_send, p_recv, dom, a)

    def local_part(i, carry):
        a = mod(blk + 1 + i, NB)
        dst_hot = hot(dst_ref[a], ROWS)
        src_hot = hot(src_ref[a], ROWS)
        count = lax.dot_general(dst_hot, src_hot, NT, preferred_element_type=F32).astype(BF16)
        counts_t[a] = lax.dot_general(src_hot, dst_hot, NT, preferred_element_type=F32).astype(BF16)
        part = jnp.dot(count, xrow[z, c], preferred_element_type=F32)

        @pl.when(i < NB - 1)
        def _():
            psend[a] = part.astype(BF16)
            part_copy(a).start()

        @pl.when(i == NB - 1)
        def _():
            own_part[...] = part
            precv[a] = jnp.zeros((ROWS, FIN), BF16)

        return carry

    lax.fori_loop(0, NB, local_part, 0)

    taken(mid.at[c, pl.ds(0, ZN - 1)], i_send.at[0], i_recv.at[0]).wait_recv()
    table_relay.start()
    taken(ya.at[pl.ds(0, YH - 1)], i_send.at[1], i_recv.at[1]).wait_recv()
    remote(mid.at[1 - c], mid.at[1 - c], i_send.at[2], i_recv.at[2], dom, blk).wait_recv()

    line_loop(xrow, xs_send, xs_recv, mf, lambda j, zz: build(mf, zz, True))
    taken(precv.at[pl.ds(0, NB - 1)], p_send, p_recv).wait_recv()
    sum_sends(hout, hin, 0)

    def build_back(zz, carry):
        build(mb, zz, False)
        return carry

    lax.fori_loop(0, ZN, build_back, 0)
    total = hacc[y] + own_part[...]
    for i in range(NB):
        total = total + precv[i].astype(F32)
    sums(hin, 0).wait_recv()
    for i in range(YH):
        total = total + hin[i].astype(F32)

    for i in (7, 8, 9):
        incoming[i].wait()
    weight = weight_ref[...]
    pre = scale * jnp.dot(total.astype(BF16), weight, preferred_element_type=F32) + bias_ref[...]
    sig = jax.nn.sigmoid(pre)
    grad_pre = cot_ref[...].astype(F32) * sig * (1.0 + pre * (1.0 - sig))
    back = (scale * grad_pre).astype(BF16)
    grad = lax.dot_general(back, weight, NT, preferred_element_type=F32).astype(BF16)
    bias_term = jnp.sum(grad_pre, axis=0, keepdims=True)
    gw = jnp.dot(total.T.astype(BF16), back, preferred_element_type=F32)
    grow[z, c] = grad
    line_sends(grow, gs_send, gs_recv)
    me_a = blk * CN + c
    me_b = y * ZN + z
    for a in range(16):
        w1s[a, 0:8, :] = gw[8 * a : 8 * a + 8, 0:128]
        w1s[a, 8:16, :] = gw[8 * a : 8 * a + 8, 128:256]
        w1s[a, 16:17, :] = bias_term[:, 0:128]
        w1s[a, 17:18, :] = bias_term[:, 128:256]
    w1r[me_a] = w1s[me_a]

    def peer_a(step):
        dx, flip, cross = step
        to_blk = mod(lax.div(blk, 2) + dx, 4) * 2 + (1 - lax.rem(blk, 2) if flip else lax.rem(blk, 2))
        to_c = 1 - c if cross else c
        return to_blk * CN + to_c, at(y, z, to_c), to_blk

    def peer_b(step):
        dy, dz = step
        return at(mod(y + dy, YH), mod(z + dz, ZN), c), blk

    gw_piece = gw_hbm.at[pl.ds(pl.multiple_of(me_a * 8, 8), 8)]
    own_piece = pltpu.make_async_copy(w3r.at[me_a], gw_piece, out_sem.at[2])

    def w1_copy(i):
        a, to_dom, to_blk = peer_a(i)
        return remote(w1s.at[a], w1r.at[me_a], w_send.at[0], w_recv.at[0], to_dom, to_blk)

    def w2_copies(i):
        return [
            remote(ref.at[me_b], ref.at[me_b], w_send.at[k], w_recv.at[k], *peer_b(i)) for ref, k in ((w2r, 1), (w2b, 3))
        ]

    def w3_copy(i):
        _, to_dom, to_blk = peer_a(i)
        return remote(w3r.at[me_a], gw_piece, w_send.at[2], w_recv.at[2], to_dom, to_blk)

    def second():
        others(w1r, 16, 0).wait_recv()
        summed = jnp.sum(w1r[...], axis=0)
        w2r[me_b] = summed[0:16].astype(BF16)
        w2b[me_b] = summed[16:18]
        for step in FAR_B:
            w2_copies(step)[0].start()
        for step in FAR_B:
            w2_copies(step)[1].start()

    def third():
        others(w2r, 32, 1).wait_recv()
        summed = jnp.sum(w2r[...].astype(F32), axis=0)
        w3r[me_a] = jnp.concatenate([summed[0:8], summed[8:16]], axis=1)
        for step in FAR_A:
            w3_copy(step).start()
        own_piece.start()
        others(w2b, 32, 3).wait_recv()
        gb_ref[...] = jnp.sum(w2b[...], axis=0)
        outgoing[2].start()

    gblk[blk] = grad

    def member_copy(i):
        return remote(grow.at[z, c], gblk.at[blk], q_send, q_recv, dom, mod(blk + i, NB))

    def others(ref, count, which):
        return taken(ref.at[pl.ds(0, count - 1)], w_send.at[which], w_recv.at[which])

    for step in FAR_A:
        w1_copy(step).start()
    each(NB, lambda i: member_copy(i).start())
    act_ref[...] = (pre * sig).astype(BF16)
    outgoing[0].start()

    def backward_extra(j, zz):
        @pl.when(j == 2)
        def _():
            second()

    line_loop(grow, gs_send, gs_recv, mb, backward_extra)
    sum_sends(bout, bin_, 1)

    third()
    taken(gblk.at[pl.ds(0, NB - 1)], q_send, q_recv).wait_recv()
    total_back = hacc[y]
    for a in range(NB):
        total_back = total_back + jnp.dot(counts_t[a], gblk[a], preferred_element_type=F32)

    sums(bin_, 1).wait_recv()
    for i in range(YH):
        total_back = total_back + bin_[i].astype(F32)
    gfeat_ref[...] = (scale * total_back).astype(BF16)
    outgoing[1].start()

    others(w3r, 16, 2).wait_recv()
    for send, recv in ((xs_send, xs_recv), (gs_send, gs_recv)):
        taken(psend.at[pl.ds(0, ZN - 1)], send.at[0], recv.at[0, 0]).wait_send()
        taken(psend, send.at[1], recv.at[0, 0]).wait_send()
    taken(mid.at[c, pl.ds(0, ZN - 1)], i_send.at[0], i_recv.at[0]).wait_send()
    taken(ya.at[pl.ds(0, YH - 1)], i_send.at[1], i_recv.at[1]).wait_send()
    table_relay.wait_send()
    sums(hin, 0).wait_send()
    sums(bin_, 1).wait_send()
    taken(precv.at[pl.ds(0, NB - 1)], p_send, p_recv).wait_send()
    taken(gblk.at[pl.ds(0, NB - 1)], q_send, q_recv).wait_send()
    others(w1r, 16, 0).wait_send()
    others(w2r, 32, 1).wait_send()
    others(w2b, 32, 3).wait_send()
    others(w3r, 16, 2).wait_send()
    own_piece.wait()
    for copy in outgoing:
        copy.wait()


def write_kernel(act, gfeat, gw, gb, act_out, gfeat_out, gw_out, gb_out, act_v, gfeat_v, gw_v, gb_v, sem):
    through = ((gw, gw_v, gw_out), (act, act_v, act_out), (gfeat, gfeat_v, gfeat_out), (gb, gb_v, gb_out))
    reads = [pltpu.make_async_copy(src, mid, sem.at[i]) for i, (src, mid, dst) in enumerate(through)]
    writes = [pltpu.make_async_copy(mid, dst, sem.at[4 + i]) for i, (src, mid, dst) in enumerate(through)]
    for copy in reads:
        copy.start()
    for read, write in zip(reads, writes):
        read.wait()
        write.start()
    for copy in writes:
        copy.wait()


def per_device(features, weight, out_bias, degree, edge_dst, edge_src, hub_rows, hub_count, hub_target, cotangent):
    hbm = pl.BlockSpec(memory_space=pltpu.HBM)
    dma = pltpu.SemaphoreType.DMA
    shapes = (
        jax.ShapeDtypeStruct((ROWS, HID), BF16),
        jax.ShapeDtypeStruct((ROWS, FIN), BF16),
        jax.ShapeDtypeStruct((FIN, HID), F32),
        jax.ShapeDtypeStruct((2, 128), F32),
    )
    results = pl.pallas_call(
        kernel,
        out_shape=shapes,
        in_specs=[hbm] * 10,
        out_specs=(hbm,) * 4,
        scratch_shapes=[
            pltpu.VMEM((ROWS, FIN), BF16),
            pltpu.VMEM((FIN, HID), BF16),
            pltpu.VMEM((1, HID), F32),
            pltpu.VMEM((1, ROWS), jnp.int32),
            pltpu.VMEM((NB, 1, EB), jnp.int32),
            pltpu.VMEM((NB, 1, EB), jnp.int32),
            pltpu.VMEM((HUB, HUB), jnp.int32),
            pltpu.VMEM((1, HUB), jnp.int32),
            pltpu.VMEM((HUB, HUB), jnp.int32),
            pltpu.VMEM((ROWS, HID), BF16),
            pltpu.VMEM((ROWS, HID), BF16),
            pltpu.VMEM((ROWS, FIN), BF16),
            pltpu.VMEM((2, 128), F32),
            pltpu.VMEM((ZN, CN, ROWS, FIN), BF16),
            pltpu.VMEM((ZN, CN, ROWS, FIN), BF16),
            pltpu.VMEM((YH, ROWS, FIN), F32),
            pltpu.VMEM((YH, ROWS, FIN), BF16),
            pltpu.VMEM((YH, ROWS, FIN), BF16),
            pltpu.VMEM((YH, ROWS, FIN), BF16),
            pltpu.VMEM((YH, ROWS, FIN), BF16),
            pltpu.VMEM((ROWS, FIN), F32),
            pltpu.VMEM((NB, ROWS, ROWS), BF16),
            pltpu.VMEM((NB, ROWS, FIN), BF16),
            pltpu.VMEM((NB, ROWS, FIN), BF16),
            pltpu.VMEM((NB, ROWS, FIN), BF16),
            pltpu.VMEM((ZN, YH * CN, 1, 2 * HUB), jnp.int32),
            pltpu.VMEM((YH, ZN * CN, 2 * HUB), jnp.int32),
            pltpu.VMEM((CN, ZN, YH * CN, 1, 2 * HUB), jnp.int32),
            pltpu.VMEM((YH, ZN * CN, 2 * HUB), jnp.int32),
            pltpu.VMEM((ZN, YH, ROWS, CN * ROWS), BF16),
            pltpu.VMEM((ZN, YH, ROWS, CN * ROWS), BF16),
            pltpu.VMEM((16, 18, 128), F32),
            pltpu.VMEM((16, 18, 128), F32),
            pltpu.VMEM((32, 16, 128), BF16),
            pltpu.VMEM((32, 2, 128), F32),
            pltpu.VMEM((16, 8, HID), F32),
            dma((10,)), dma((4,)), dma((2,)), dma((ZN, CN)), dma((2,)), dma((ZN, CN)),
            dma((2,)), dma((2,)), dma(()), dma(()), dma(()), dma(()), dma((3,)), dma((3,)), dma((4,)), dma((4,)),
        ],
        compiler_params=pltpu.CompilerParams(
            collective_id=0, has_side_effects=True, vmem_limit_bytes=60 * 1024 * 1024
        ),
    )(
        features, weight, out_bias.reshape(1, HID), degree.reshape(1, ROWS), edge_dst, edge_src,
        hub_rows, hub_count, hub_target, cotangent,
    )
    act, gfeat, gw, gb = pl.pallas_call(
        write_kernel,
        out_shape=shapes,
        in_specs=[hbm] * 4,
        out_specs=(hbm,) * 4,
        scratch_shapes=[pltpu.VMEM(shape.shape, shape.dtype) for shape in shapes] + [dma((8,))],
        compiler_params=pltpu.CompilerParams(vmem_limit_bytes=60 * 1024 * 1024),
    )(*results)
    return act, gfeat, gw, gb.reshape(HID)


def solution(mesh):
    return jax.shard_map(
        per_device,
        mesh=mesh,
        in_specs=(
            P(("dom", "blk"), None),
            P(),
            P(),
            P(("dom", "blk")),
            P("dom", "blk", None),
            P("dom", "blk", None),
            P("dom", "blk", None, None),
            P("dom", "blk", None),
            P("dom", "blk", None, None),
            P(("dom", "blk"), None),
        ),
        out_specs=(P(("dom", "blk"), None), P(("dom", "blk"), None), P(), P()),
        check_vma=False,
    )
```

```python
import functools

import jax
import jax.numpy as jnp
from jax import lax
from jax.experimental import pallas as pl
from jax.experimental.pallas import tpu as pltpu
from jax.sharding import PartitionSpec as P

F32 = jnp.float32
BF16 = jnp.bfloat16
NT = (((1,), (1,)), ((), ()))
YH, ZN, CN, NB = 4, 8, 2, 8
ROWS, FIN, HID, HUB, EB = 128, 128, 256, 64, 384


def ring(step, size):
    return min(step, size - step)


FAR_A = sorted(
    ((dx, flip, cross) for dx in range(4) for flip in range(2) for cross in range(CN) if dx or flip or cross),
    key=lambda step: -(ring(step[0], 4) + step[1]),
)
FAR_B = sorted(
    ((dy, dz) for dy in range(YH) for dz in range(ZN) if dy or dz),
    key=lambda step: -(2 * ring(step[0], YH) + ring(step[1], ZN)),
)


def iota(shape, dim):
    return lax.broadcasted_iota(jnp.int32, shape, dim)


def mod(value, size):
    return lax.rem(value + size, size)


def column(row):
    n = row.shape[1]
    wide = jnp.broadcast_to(row.astype(F32), (n, n))
    return jnp.sum(jnp.where(iota((n, n), 0) == iota((n, n), 1), wide, 0.0), axis=1, keepdims=True)


def hot(row, size):
    return (iota((size, row.shape[1]), 0) == row).astype(F32).astype(BF16)


def kernel(
    feat_hbm, weight_hbm, bias_hbm, degree_hbm, dst_hbm, src_hbm, rows_hbm, count_hbm, target_hbm, cot_hbm,
    act_hbm, gfeat_hbm, gw_hbm, gb_hbm,
    feat_ref, weight_ref, bias_ref, degree_ref, dst_ref, src_ref, rows_ref, count_ref, target_ref, cot_ref,
    act_ref, gfeat_ref, gb_ref,
    xrow, grow, hacc, hout, hin, bout, bin_, own_part, counts_t, psend, precv, gblk, sendtab, loctab, mid, ya, mf, mb,
    w1s, w1r, w2r, w2b, w3r,
    in_sem, out_sem, xs_send, xs_recv, gs_send, gs_recv, h_send, h_recv, p_send, p_recv, q_send, q_recv,
    i_send, i_recv, w_send, w_recv,
):
    dom = lax.axis_index("dom")
    blk = lax.axis_index("blk")
    c = lax.rem(dom, CN)
    z = lax.rem(lax.div(dom, CN), ZN)
    y = lax.div(dom, CN * ZN)

    def at(yy, zz, cc):
        return (yy * ZN + zz) * CN + cc

    def each(count, body):
        def run(i, carry):
            body(i)
            return carry

        lax.fori_loop(1, count, run, 0)

    barrier = pltpu.get_barrier_semaphore()

    def greet(to_dom, to_blk):
        pl.semaphore_signal(barrier, inc=1, device_id=(to_dom, to_blk), device_id_type=pl.DeviceIdType.MESH)

    for i in range(1, ZN):
        greet(at(y, mod(z + i, ZN), c), blk)
    for i in range(1, YH):
        greet(at(mod(y + i, YH), z, c), blk)
    for i in range(1, NB * CN):
        a = mod(blk * CN + c + i, NB * CN)
        greet(at(y, z, lax.rem(a, CN)), lax.div(a, CN))

    incoming = [
        pltpu.make_async_copy(src, dst, in_sem.at[i])
        for i, (src, dst) in enumerate(
            (
                (degree_hbm, degree_ref), (feat_hbm, feat_ref), (count_hbm.at[0], count_ref),
                (rows_hbm.at[0, 0], rows_ref), (target_hbm.at[0, 0], target_ref), (dst_hbm, dst_ref),
                (src_hbm, src_ref), (weight_hbm, weight_ref), (bias_hbm, bias_ref), (cot_hbm, cot_ref),
            )
        )
    ]
    for copy in incoming:
        copy.start()

    outgoing = [
        pltpu.make_async_copy(src, dst, out_sem.at[3 if i == 2 else i])
        for i, (src, dst) in enumerate(
            ((act_ref, act_hbm), (gfeat_ref, gfeat_hbm), (gb_ref, gb_hbm))
        )
    ]

    def remote(src, dst, send, recv, to_dom, to_blk):
        return pltpu.make_async_remote_copy(
            src_ref=src, dst_ref=dst, send_sem=send, recv_sem=recv,
            device_id=(to_dom, to_blk), device_id_type=pl.DeviceIdType.MESH,
        )

    def taken(ref, send, recv):
        return remote(ref, ref, send, recv, dom, blk)

    incoming[0].wait()
    incoming[1].wait()
    scale = lax.rsqrt(column(degree_ref[...]))
    xrow[z, c] = (scale * feat_ref[...].astype(F32)).astype(BF16)

    for i in (2, 3, 4):
        incoming[i].wait()
    live = iota((HUB, HUB), 1).astype(F32) < column(count_ref[...])
    rows = jnp.where(live, rows_ref[...], ROWS)
    target = target_ref[...]
    joint_tab = jnp.concatenate([rows, target], axis=1)
    loctab[...] = jnp.concatenate([target, rows], axis=1).reshape(YH, ZN * CN, 2 * HUB)
    for e in range(YH * ZN * CN):
        sendtab[(e // CN) % ZN, (e // (CN * ZN)) * CN + e % CN] = joint_tab[e : e + 1, :]

    def table_z(i):
        zz = mod(z + i, ZN)
        return remote(sendtab.at[zz], mid.at[c, z], i_send.at[0], i_recv.at[0], at(y, zz, c), blk)

    def table_y(i):
        yy = mod(y + i, YH)
        return remote(loctab.at[yy], ya.at[y], i_send.at[1], i_recv.at[1], at(yy, z, c), blk)

    table_relay = remote(mid.at[c], mid.at[c], i_send.at[2], i_recv.at[2], at(y, z, 1 - c), blk)

    def block_copy(buf, send, recv, zz, cc, to_dom, kind=0):
        return remote(buf.at[zz, cc], buf.at[zz, cc], send.at[kind], recv.at[zz, cc], to_dom, blk)

    def distance(j):
        half = lax.div(j + 1, 2)
        return jnp.where(lax.rem(j, 2) == 1, half, ZN - half)

    def line_sends(buf, send, recv):
        for i in (1, 7, 2, 6, 3, 5, 4):
            block_copy(buf, send, recv, z, c, at(y, mod(z + i, ZN), c)).start()
        block_copy(buf, send, recv, z, c, at(y, z, 1 - c), 1).start()

    def build(counts, zz, forward):
        keep = (iota((1, 2 * HUB), 1) < HUB) == forward
        for yy in range(YH):
            for cc in range(CN):
                mine = jnp.where(keep, ya[yy, pl.ds(zz * CN + cc, 1), :], -1)
                theirs = mid[cc, zz, yy * CN + c]
                counts[zz, yy, :, cc * ROWS : (cc + 1) * ROWS] = lax.dot_general(
                    hot(mine, ROWS), hot(theirs, ROWS), NT, preferred_element_type=F32
                ).astype(BF16)

    def line_loop(buf, send, recv, counts, prepare):
        hacc[...] = jnp.zeros_like(hacc)

        def step(j, carry):
            zz = mod(z + distance(j), ZN)
            prepare(j, zz)

            @pl.when(j < ZN - 1)
            def _():
                after = mod(z + distance(j + 1), ZN)
                block_copy(buf, send, recv, after, c, dom).wait_recv()
                block_copy(buf, send, recv, after, c, at(y, z, 1 - c), 1).start()

            block_copy(buf, send, recv, zz, 1 - c, dom).wait_recv()
            part = jnp.dot(
                counts[zz].reshape(YH * ROWS, CN * ROWS), buf[zz].reshape(CN * ROWS, FIN), preferred_element_type=F32
            )
            hacc[...] += part.reshape(YH, ROWS, FIN)
            return carry

        lax.fori_loop(0, ZN, step, 0)

    def sum_sends(out, inn, which):
        for i in (2, 1, 3):
            yy = mod(y + i, YH)
            out[yy] = hacc[yy].astype(BF16)
            remote(out.at[yy], inn.at[y], h_send.at[which], h_recv.at[which], at(yy, z, c), blk).start()
        inn[y] = jnp.zeros((ROWS, FIN), BF16)

    def sums(inn, which):
        return taken(inn.at[pl.ds(0, YH - 1)], h_send.at[which], h_recv.at[which])

    pl.semaphore_wait(barrier, (NB * CN - 1) + (ZN - 1) + (YH - 1))

    for i in (4, 3, 5, 2, 6, 1, 7):
        table_z(i).start()
    for i in (2, 1, 3):
        table_y(i).start()
    line_sends(xrow, xs_send, xs_recv)
    mid[c, z] = sendtab[z]
    ya[y] = loctab[y]

    incoming[5].wait()
    incoming[6].wait()

    def part_copy(a):
        return remote(psend.at[a], precv.at[blk], p_send, p_recv, dom, a)

    def local_part(i, carry):
        @pl.when(i == 4)
        def _():
            taken(mid.at[c, pl.ds(0, ZN - 1)], i_send.at[0], i_recv.at[0]).wait_recv()
            table_relay.start()

        a = mod(blk + 1 + i, NB)
        dst_hot = hot(dst_ref[a], ROWS)
        src_hot = hot(src_ref[a], ROWS)
        count = lax.dot_general(dst_hot, src_hot, NT, preferred_element_type=F32).astype(BF16)
        counts_t[a] = lax.dot_general(src_hot, dst_hot, NT, preferred_element_type=F32).astype(BF16)
        part = jnp.dot(count, xrow[z, c], preferred_element_type=F32)

        @pl.when(i < NB - 1)
        def _():
            psend[a] = part.astype(BF16)
            part_copy(a).start()

        @pl.when(i == NB - 1)
        def _():
            own_part[...] = part
            precv[a] = jnp.zeros((ROWS, FIN), BF16)

        return carry

    lax.fori_loop(0, NB, local_part, 0)

    taken(ya.at[pl.ds(0, YH - 1)], i_send.at[1], i_recv.at[1]).wait_recv()
    remote(mid.at[1 - c], mid.at[1 - c], i_send.at[2], i_recv.at[2], dom, blk).wait_recv()

    line_loop(xrow, xs_send, xs_recv, mf, lambda j, zz: build(mf, zz, True))
    taken(precv.at[pl.ds(0, NB - 1)], p_send, p_recv).wait_recv()
    sum_sends(hout, hin, 0)

    def build_back(zz, carry):
        build(mb, zz, False)
        return carry

    lax.fori_loop(0, ZN, build_back, 0)
    total = hacc[y] + own_part[...]
    for i in range(NB):
        total = total + precv[i].astype(F32)
    sums(hin, 0).wait_recv()
    for i in range(YH):
        total = total + hin[i].astype(F32)

    for i in (7, 8, 9):
        incoming[i].wait()
    weight = weight_ref[...]
    pre = scale * jnp.dot(total.astype(BF16), weight, preferred_element_type=F32) + bias_ref[...]
    sig = jax.nn.sigmoid(pre)
    grad_pre = cot_ref[...].astype(F32) * sig * (1.0 + pre * (1.0 - sig))
    back = (scale * grad_pre).astype(BF16)
    grad = lax.dot_general(back, weight, NT, preferred_element_type=F32).astype(BF16)
    bias_term = jnp.sum(grad_pre, axis=0, keepdims=True)
    gw = jnp.dot(total.T.astype(BF16), back, preferred_element_type=F32)
    grow[z, c] = grad
    line_sends(grow, gs_send, gs_recv)
    me_a = blk * CN + c
    me_b = y * ZN + z
    for a in range(16):
        w1s[a, 0:8, :] = gw[8 * a : 8 * a + 8, 0:128]
        w1s[a, 8:16, :] = gw[8 * a : 8 * a + 8, 128:256]
        w1s[a, 16:17, :] = bias_term[:, 0:128]
        w1s[a, 17:18, :] = bias_term[:, 128:256]
    w1r[me_a] = w1s[me_a]

    def peer_a(step):
        dx, flip, cross = step
        to_blk = mod(lax.div(blk, 2) + dx, 4) * 2 + (1 - lax.rem(blk, 2) if flip else lax.rem(blk, 2))
        to_c = 1 - c if cross else c
        return to_blk * CN + to_c, at(y, z, to_c), to_blk

    def peer_b(step):
        dy, dz = step
        return at(mod(y + dy, YH), mod(z + dz, ZN), c), blk

    gw_piece = gw_hbm.at[pl.ds(pl.multiple_of(me_a * 8, 8), 8)]
    own_piece = pltpu.make_async_copy(w3r.at[me_a], gw_piece, out_sem.at[2])

    def w1_copy(i):
        a, to_dom, to_blk = peer_a(i)
        return remote(w1s.at[a], w1r.at[me_a], w_send.at[0], w_recv.at[0], to_dom, to_blk)

    def w2_copies(i):
        return [
            remote(ref.at[me_b], ref.at[me_b], w_send.at[k], w_recv.at[k], *peer_b(i)) for ref, k in ((w2r, 1), (w2b, 3))
        ]

    def w3_copy(i):
        _, to_dom, to_blk = peer_a(i)
        return remote(w3r.at[me_a], gw_piece, w_send.at[2], w_recv.at[2], to_dom, to_blk)

    def second():
        others(w1r, 16, 0).wait_recv()
        summed = jnp.sum(w1r[...], axis=0)
        w2r[me_b] = summed[0:16].astype(BF16)
        w2b[me_b] = summed[16:18]
        for step in FAR_B:
            w2_copies(step)[0].start()
        for step in FAR_B:
            w2_copies(step)[1].start()

    def third():
        others(w2r, 32, 1).wait_recv()
        summed = jnp.sum(w2r[...].astype(F32), axis=0)
        w3r[me_a] = jnp.concatenate([summed[0:8], summed[8:16]], axis=1)
        for step in FAR_A:
            w3_copy(step).start()
        own_piece.start()
        others(w2b, 32, 3).wait_recv()
        gb_ref[...] = jnp.sum(w2b[...], axis=0)
        outgoing[2].start()

    gblk[blk] = grad

    def member_copy(i):
        return remote(grow.at[z, c], gblk.at[blk], q_send, q_recv, dom, mod(blk + i, NB))

    def others(ref, count, which):
        return taken(ref.at[pl.ds(0, count - 1)], w_send.at[which], w_recv.at[which])

    for step in FAR_A:
        w1_copy(step).start()
    each(NB, lambda i: member_copy(i).start())
    act_ref[...] = (pre * sig).astype(BF16)
    outgoing[0].start()

    def backward_extra(j, zz):
        @pl.when(j == 2)
        def _():
            second()

    line_loop(grow, gs_send, gs_recv, mb, backward_extra)
    sum_sends(bout, bin_, 1)

    third()
    taken(gblk.at[pl.ds(0, NB - 1)], q_send, q_recv).wait_recv()
    total_back = hacc[y]
    for a in range(NB):
        total_back = total_back + jnp.dot(counts_t[a], gblk[a], preferred_element_type=F32)

    sums(bin_, 1).wait_recv()
    for i in range(YH):
        total_back = total_back + bin_[i].astype(F32)
    gfeat_ref[...] = (scale * total_back).astype(BF16)
    outgoing[1].start()

    others(w3r, 16, 2).wait_recv()
    for send, recv in ((xs_send, xs_recv), (gs_send, gs_recv)):
        taken(psend.at[pl.ds(0, ZN - 1)], send.at[0], recv.at[0, 0]).wait_send()
        taken(psend, send.at[1], recv.at[0, 0]).wait_send()
    taken(mid.at[c, pl.ds(0, ZN - 1)], i_send.at[0], i_recv.at[0]).wait_send()
    taken(ya.at[pl.ds(0, YH - 1)], i_send.at[1], i_recv.at[1]).wait_send()
    table_relay.wait_send()
    sums(hin, 0).wait_send()
    sums(bin_, 1).wait_send()
    taken(precv.at[pl.ds(0, NB - 1)], p_send, p_recv).wait_send()
    taken(gblk.at[pl.ds(0, NB - 1)], q_send, q_recv).wait_send()
    others(w1r, 16, 0).wait_send()
    others(w2r, 32, 1).wait_send()
    others(w2b, 32, 3).wait_send()
    others(w3r, 16, 2).wait_send()
    own_piece.wait()
    for copy in outgoing:
        copy.wait()


def write_kernel(act, gfeat, gw, gb, act_out, gfeat_out, gw_out, gb_out, act_v, gfeat_v, gw_v, gb_v, sem):
    through = ((gw, gw_v, gw_out), (act, act_v, act_out), (gfeat, gfeat_v, gfeat_out), (gb, gb_v, gb_out))
    reads = [pltpu.make_async_copy(src, mid, sem.at[i]) for i, (src, mid, dst) in enumerate(through)]
    writes = [pltpu.make_async_copy(mid, dst, sem.at[4 + i]) for i, (src, mid, dst) in enumerate(through)]
    for copy in reads:
        copy.start()
    for read, write in zip(reads, writes):
        read.wait()
        write.start()
    for copy in writes:
        copy.wait()


def per_device(features, weight, out_bias, degree, edge_dst, edge_src, hub_rows, hub_count, hub_target, cotangent):
    hbm = pl.BlockSpec(memory_space=pltpu.HBM)
    dma = pltpu.SemaphoreType.DMA
    shapes = (
        jax.ShapeDtypeStruct((ROWS, HID), BF16),
        jax.ShapeDtypeStruct((ROWS, FIN), BF16),
        jax.ShapeDtypeStruct((FIN, HID), F32),
        jax.ShapeDtypeStruct((2, 128), F32),
    )
    results = pl.pallas_call(
        kernel,
        out_shape=shapes,
        in_specs=[hbm] * 10,
        out_specs=(hbm,) * 4,
        scratch_shapes=[
            pltpu.VMEM((ROWS, FIN), BF16),
            pltpu.VMEM((FIN, HID), BF16),
            pltpu.VMEM((1, HID), F32),
            pltpu.VMEM((1, ROWS), jnp.int32),
            pltpu.VMEM((NB, 1, EB), jnp.int32),
            pltpu.VMEM((NB, 1, EB), jnp.int32),
            pltpu.VMEM((HUB, HUB), jnp.int32),
            pltpu.VMEM((1, HUB), jnp.int32),
            pltpu.VMEM((HUB, HUB), jnp.int32),
            pltpu.VMEM((ROWS, HID), BF16),
            pltpu.VMEM((ROWS, HID), BF16),
            pltpu.VMEM((ROWS, FIN), BF16),
            pltpu.VMEM((2, 128), F32),
            pltpu.VMEM((ZN, CN, ROWS, FIN), BF16),
            pltpu.VMEM((ZN, CN, ROWS, FIN), BF16),
            pltpu.VMEM((YH, ROWS, FIN), F32),
            pltpu.VMEM((YH, ROWS, FIN), BF16),
            pltpu.VMEM((YH, ROWS, FIN), BF16),
            pltpu.VMEM((YH, ROWS, FIN), BF16),
            pltpu.VMEM((YH, ROWS, FIN), BF16),
            pltpu.VMEM((ROWS, FIN), F32),
            pltpu.VMEM((NB, ROWS, ROWS), BF16),
            pltpu.VMEM((NB, ROWS, FIN), BF16),
            pltpu.VMEM((NB, ROWS, FIN), BF16),
            pltpu.VMEM((NB, ROWS, FIN), BF16),
            pltpu.VMEM((ZN, YH * CN, 1, 2 * HUB), jnp.int32),
            pltpu.VMEM((YH, ZN * CN, 2 * HUB), jnp.int32),
            pltpu.VMEM((CN, ZN, YH * CN, 1, 2 * HUB), jnp.int32),
            pltpu.VMEM((YH, ZN * CN, 2 * HUB), jnp.int32),
            pltpu.VMEM((ZN, YH, ROWS, CN * ROWS), BF16),
            pltpu.VMEM((ZN, YH, ROWS, CN * ROWS), BF16),
            pltpu.VMEM((16, 18, 128), F32),
            pltpu.VMEM((16, 18, 128), F32),
            pltpu.VMEM((32, 16, 128), BF16),
            pltpu.VMEM((32, 2, 128), F32),
            pltpu.VMEM((16, 8, HID), F32),
            dma((10,)), dma((4,)), dma((2,)), dma((ZN, CN)), dma((2,)), dma((ZN, CN)),
            dma((2,)), dma((2,)), dma(()), dma(()), dma(()), dma(()), dma((3,)), dma((3,)), dma((4,)), dma((4,)),
        ],
        compiler_params=pltpu.CompilerParams(
            collective_id=0, has_side_effects=True, vmem_limit_bytes=60 * 1024 * 1024
        ),
    )(
        features, weight, out_bias.reshape(1, HID), degree.reshape(1, ROWS), edge_dst, edge_src,
        hub_rows, hub_count, hub_target, cotangent,
    )
    act, gfeat, gw, gb = pl.pallas_call(
        write_kernel,
        out_shape=shapes,
        in_specs=[hbm] * 4,
        out_specs=(hbm,) * 4,
        scratch_shapes=[pltpu.VMEM(shape.shape, shape.dtype) for shape in shapes] + [dma((8,))],
        compiler_params=pltpu.CompilerParams(vmem_limit_bytes=60 * 1024 * 1024),
    )(*results)
    return act, gfeat, gw, gb.reshape(HID)


def solution(mesh):
    return jax.shard_map(
        per_device,
        mesh=mesh,
        in_specs=(
            P(("dom", "blk"), None),
            P(),
            P(),
            P(("dom", "blk")),
            P("dom", "blk", None),
            P("dom", "blk", None),
            P("dom", "blk", None, None),
            P("dom", "blk", None),
            P("dom", "blk", None, None),
            P(("dom", "blk"), None),
        ),
        out_specs=(P(("dom", "blk"), None), P(("dom", "blk"), None), P(), P()),
        check_vma=False,
    )
```
